32 devices in a mesh: section: 4 (over x, core), expert: 4 (over z), dp: 2 (over y).
Axes of the slice: x: 2, y: 2, z: 4, core: 2. Of those that a mesh axis runs over, the one named last changes fastest.
Arguments:
- fwd_sent: bfloat16 [4, 128, 3584], P('section', ('expert', 'dp')), may hold values from -6 to 6
- fwd_routes: int32 [4, 128, 1], P('section', ('expert', 'dp')), may hold values from 0 to 1; in each aligned block of 16 rows (0 to 15, 16 to 31, ..., all dimensions but the last counted through in order) at most 16 rows name the same one
- fwd_probs: float32 [4, 128, 1], P('section', ('expert', 'dp')), may hold values from 0.2 to 1.25
- backward_cotangent: bfloat16 [4, 128, 3584], P('section', ('expert', 'dp')), may hold values from -6 to 6
- bwd_routes: int32 [4, 128, 1], P('section', ('expert', 'dp')), may hold values from 0 to 1; in each aligned block of 16 rows (0 to 15, 16 to 31, ..., all dimensions but the last counted through in order) at most 16 rows name the same one
- bwd_probs: float32 [4, 128, 1], P('section', ('expert', 'dp')), may hold values from 0.2 to 1.25
- saved_pre: bfloat16 [4, 2, 64, 2, 2048], P('section', 'dp', None, None, 'expert'), may hold values from -6 to 6
- w_gate: bfloat16 [4, 3584, 2048], P('section', None, 'expert'), may hold values from -0.09375 to 0.09375
- w_up: bfloat16 [4, 3584, 2048], P('section', None, 'expert'), may hold values from -0.09375 to 0.09375
- w_down: bfloat16 [4, 2048, 3584], P('section', 'expert'), may hold values from -0.1875 to 0.1875
Outputs:
- fwd_next: bfloat16 [4, 128, 3584], P('section', ('expert', 'dp'))
- bwd_next: bfloat16 [4, 128, 3584], P('section', ('expert', 'dp'))
- expert_load: int32 [4, 4], P('section', 'expert')
The draws below stay inside these ranges and needn't reach their ends.
Inputs may be any that keep to these rules, and one draw needn't show every extreme that they name: `fwd_routes`: among the rows of one device, no expert is named by more than 16 routes, a bound that some block reaches; a row names 1 different experts. `bwd_routes`: among the rows of one device, no expert is named by more than 16 routes, a bound that some block reaches; a row names 1 different experts.
All inputs are finite; a program needn't handle non-finite values.
Results may differ from the reference program's by a relative error of at most 0.007.
Values may be sent and summed in bfloat16 or wider, within the bound.
A program may use at most 64 MiB of HBM per device.

```python
import math
import jax
import jax.numpy as jnp
import numpy as np
from jax import lax

D = 3584
FF = 1024
TOPK = 1
TOK_DEV = 16
SHARD_GROUP = 2
EXP = 2
HIDDEN_PER_UNIT = 512
CAP = 16
TOKENS = 128
SLOT_CAPACITY = 64
N_SECTION = 4
N_EXPERT = 4
N_DP = 2


def levels(own_key, dims, cuts, smallest, largest):
    factor_of, own = 1.0, jax.random.fold_in(own_key, 6)
    for axis_at, parts in cuts:
        steps = jnp.exp(jax.random.uniform(jax.random.fold_in(own, axis_at), (parts,), jnp.float32, smallest / len(cuts), largest / len(cuts)))
        factor_of = factor_of * jnp.repeat(steps, dims[axis_at] // parts).reshape([-1 if axis == axis_at else 1 for axis in range(len(dims))])
    return factor_of


def routed_block(key, own, number, rows, number_of, top, reach, slope):
    ranking = jax.random.permutation(key, number_of)
    crowded, ordinary = shares(number_of, rows * top, reach, slope, True), shares(number_of, rows * top, reach, slope, False)
    places = jnp.arange(number_of)

    def named(sizes, turn):
        used = int((sizes > 0).sum())
        fixed = max(1, used // 4)
        passed = fixed + (places - fixed + turn * (used - fixed)) % max(1, number_of - fixed)
        return jnp.zeros((number_of,), jnp.int32).at[ranking[jnp.where(places < fixed, places, passed)]].set(jnp.asarray(sizes, jnp.int32))

    sizes = jnp.where(number % 4 == 0, named(crowded, number // 4), named(ordinary, number - number // 4 - 1))
    mixed = jax.random.permutation(jax.random.fold_in(own, 3), number_of)
    donor, sink = mixed[0:number_of // 2 * 2:2], mixed[1:number_of // 2 * 2:2]
    slack = jnp.minimum(sizes[donor] - 1, reach - sizes[sink]) // 2
    slack = jnp.where((donor == ranking[0]) | (sink == ranking[0]) | (sizes[sink] == 0), 0, jnp.maximum(slack, 0))
    passed = jax.random.randint(jax.random.fold_in(own, 4), (number_of // 2,), 0, 1 << 20) % (slack + 1)
    sizes = sizes.at[donor].add(-passed).at[sink].add(passed)
    labels = jnp.searchsorted(jnp.cumsum(sizes), jnp.arange(rows * top), side="right").astype(jnp.int32)
    table = labels.reshape(top, rows).T
    table = table[jax.random.permutation(jax.random.fold_in(own, 1), rows)]
    turn = jax.random.randint(jax.random.fold_in(own, 2), (rows, 1), 0, top)
    return jnp.take_along_axis(table, (jnp.arange(top)[None, :] + turn) % top, axis=1)


def shares(count, total, most, skew, full):
    weights = [(1 << 20) // math.isqrt(grade ** skew) + 1 for grade in range(1, count + 1)]
    largest = most if full else min(most, max(-(-total // count), total * weights[0] // sum(weights)))
    least = 1 if total - largest >= count - 1 else 0
    given, surplus = [largest] + [least] * (count - 1), total - largest - least * (count - 1)
    while surplus > 0:
        movable = [i for i in range(1, count) if given[i] < largest] or [i for i in range(1, count) if given[i] < most]
        pool, remaining = sum([weights[i] for i in movable]), surplus
        for i in movable:
            more = min(most - given[i], max(1, remaining * weights[i] // pool), surplus)
            given[i] = given[i] + more
            surplus = surplus - more
    return np.array(given)


def bell_draw(own_key, dims, scale, limit, pieces=(), kind=jnp.bfloat16):
    result = jax.random.normal(own_key, dims, jnp.float32) * scale
    if len(pieces) > 0:
        result = levels(own_key, dims, pieces, -0.22, 0.18) * result
    return jnp.clip(result, min=-limit, max=limit).astype(kind)


def setup_inputs(seed: int = 0) -> dict:
    seeds = jax.random.split(jax.random.key(seed), 11)
    fwd_sent = bell_draw(seeds[0], (N_SECTION, TOKENS, D), 1.0, 6.0, ((0, 4), (1, 8)))
    fwd_routes_keys = jax.random.split(jax.random.fold_in(seeds[1], 1), N_SECTION * TOKENS // TOK_DEV)
    fwd_routes_turns = jax.random.permutation(jax.random.fold_in(seeds[1], 3), N_SECTION * TOKENS // TOK_DEV)
    fwd_routes = jax.vmap(lambda own, number: routed_block(jax.random.fold_in(seeds[1], 2), own, number, TOK_DEV, EXP, TOPK, CAP, 2))(fwd_routes_keys, fwd_routes_turns).reshape((N_SECTION, TOKENS, TOPK))
    fwd_probs = jnp.clip(jnp.exp(math.log(1.25) - 1.8325814 * jax.random.uniform(seeds[2], (N_SECTION, TOKENS, TOPK), jnp.float32) ** levels(seeds[2], (N_SECTION, TOKENS, TOPK), ((0, 4), (1, 8)), -0.2, 0.2)), 0.2, 1.25)
    backward_cotangent = bell_draw(seeds[3], (N_SECTION, TOKENS, D), 1.0, 6.0, ((0, 4), (1, 8)))
    bwd_routes_keys = jax.random.split(jax.random.fold_in(seeds[4], 1), N_SECTION * TOKENS // TOK_DEV)
    bwd_routes_turns = jax.random.permutation(jax.random.fold_in(seeds[4], 3), N_SECTION * TOKENS // TOK_DEV)
    bwd_routes = jax.vmap(lambda own, number: routed_block(jax.random.fold_in(seeds[4], 2), own, number, TOK_DEV, EXP, TOPK, CAP, 2))(bwd_routes_keys, bwd_routes_turns).reshape((N_SECTION, TOKENS, TOPK))
    bwd_probs = jnp.clip(jnp.exp(math.log(1.25) - 1.8325814 * jax.random.uniform(seeds[5], (N_SECTION, TOKENS, TOPK), jnp.float32) ** levels(seeds[5], (N_SECTION, TOKENS, TOPK), ((0, 4), (1, 8)), -0.2, 0.2)), 0.2, 1.25)
    saved_pre = bell_draw(seeds[6], (N_SECTION, N_DP, SLOT_CAPACITY, 2, EXP * FF), 1.0, 6.0, ((0, 4), (1, 2), (4, 4)))
    w_gate = bell_draw(seeds[7], (N_SECTION, D, EXP * FF), D ** -0.5, 0.09375, ((0, 4), (2, 4)))
    w_up = bell_draw(seeds[8], (N_SECTION, D, EXP * FF), D ** -0.5, 0.09375, ((0, 4), (2, 4)))
    w_down = bell_draw(seeds[9], (N_SECTION, EXP * FF, D), FF ** -0.5, 0.1875, ((0, 4), (1, 4)))
    return dict(fwd_sent=fwd_sent, fwd_routes=fwd_routes, fwd_probs=fwd_probs, backward_cotangent=backward_cotangent, bwd_routes=bwd_routes, bwd_probs=bwd_probs, saved_pre=saved_pre, w_gate=w_gate, w_up=w_up, w_down=w_down)


def slot_tables(routes, probs):
    flat_routes = routes.reshape(-1)
    onehot = (flat_routes[:, None] == jnp.arange(EXP, dtype=jnp.int32)[None, :]).astype(jnp.int32)
    before = jnp.cumsum(onehot, axis=0) - onehot
    position = jnp.sum(before * onehot, axis=1).astype(jnp.int32)
    slot_ids = flat_routes * CAP + position
    matches = (slot_ids[:, None] == jnp.arange(EXP * CAP, dtype=jnp.int32)[None, :]).astype(jnp.float32)
    matches = matches.reshape(routes.shape[0], routes.shape[1], EXP * CAP)
    placing = jnp.sum(matches, axis=1)
    weighing = jnp.sum(matches * probs[:, :, None], axis=1)
    return placing, weighing


def dispatch(tokens, routes, probs):
    blocks = tokens.reshape(N_EXPERT, N_DP, TOK_DEV, D)
    placing, weighing = jax.vmap(jax.vmap(slot_tables))(
        routes.reshape(N_EXPERT, N_DP, TOK_DEV, TOPK), probs.reshape(N_EXPERT, N_DP, TOK_DEV, TOPK))
    buffer = jnp.einsum('jdts,jdtc->jdsc', placing, blocks.astype(jnp.float32)).astype(jnp.bfloat16)
    buffer = buffer.reshape(N_EXPERT, N_DP, EXP, CAP, D).transpose(2, 1, 0, 3, 4).reshape(EXP, N_DP, SLOT_CAPACITY, D)
    return blocks, weighing, buffer


def collect(blocks, weighing, result_list):
    returned = result_list.reshape(EXP, N_DP, N_EXPERT, CAP, D).transpose(2, 1, 0, 3, 4).reshape(N_EXPERT, N_DP, EXP * CAP, D)
    summed = blocks.astype(jnp.float32) + jnp.einsum('jdts,jdsc->jdtc', weighing, returned, precision=lax.Precision.HIGHEST)
    return summed.astype(jnp.bfloat16).reshape(TOKENS, D)


def expert_forward(inputs):
    rows_in, gate_w, up_w, down_w = inputs
    rows_in = rows_in.astype(jnp.float32)
    gate_pre = jnp.einsum('rsc,cf->rsf', rows_in, gate_w.astype(jnp.float32))
    up_pre = jnp.einsum('rsc,cf->rsf', rows_in, up_w.astype(jnp.float32))
    hidden_state = (jax.nn.silu(gate_pre) * up_pre).astype(jnp.bfloat16).astype(jnp.float32)
    partial_pieces = jnp.einsum('vtqo,qou->vtqu', hidden_state.reshape(N_DP, SLOT_CAPACITY, SHARD_GROUP, HIDDEN_PER_UNIT),
                       down_w.astype(jnp.float32).reshape(SHARD_GROUP, HIDDEN_PER_UNIT, D)).astype(jnp.bfloat16)
    return jnp.sum(partial_pieces.astype(jnp.float32), axis=2)


def expert_backward(inputs):
    rows_in, stored, gate_w, up_w, down_w = inputs
    grad_hidden = jnp.einsum('rsc,fc->rsf', rows_in.astype(jnp.float32), down_w.astype(jnp.float32))
    stored = stored.astype(jnp.float32)
    saved_gate = stored[:, :, 0]
    saved_up = stored[:, :, 1]
    sigma = jax.nn.sigmoid(saved_gate)
    grad_gate = (grad_hidden * saved_up * sigma * (1.0 + saved_gate * (1.0 - sigma))).astype(jnp.bfloat16)
    grad_up = (grad_hidden * saved_gate * sigma).astype(jnp.bfloat16)
    partial_pieces = jnp.einsum('rsgf,cgf->rsgc', grad_gate.astype(jnp.float32).reshape(N_DP, SLOT_CAPACITY, SHARD_GROUP, HIDDEN_PER_UNIT),
                       gate_w.astype(jnp.float32).reshape(D, SHARD_GROUP, HIDDEN_PER_UNIT))
    partial_pieces = partial_pieces + jnp.einsum('rsgf,cgf->rsgc', grad_up.astype(jnp.float32).reshape(N_DP, SLOT_CAPACITY, SHARD_GROUP, HIDDEN_PER_UNIT),
                               up_w.astype(jnp.float32).reshape(D, SHARD_GROUP, HIDDEN_PER_UNIT))
    return jnp.sum(partial_pieces.astype(jnp.bfloat16).astype(jnp.float32), axis=2)


def section_pass(inputs):
    x_in, f_routes, f_probs, cotangent, b_routes, b_probs, stored, gate_w, up_w, down_w = inputs
    gate_w = gate_w.reshape(D, EXP, FF).transpose(1, 0, 2)
    up_w = up_w.reshape(D, EXP, FF).transpose(1, 0, 2)
    down_w = down_w.reshape(EXP, FF, D)
    stored = stored.reshape(N_DP, SLOT_CAPACITY, 2, EXP, FF).transpose(3, 0, 1, 2, 4)
    blocks, weighing, buffer = dispatch(x_in, f_routes, f_probs)
    result_list = lax.map(expert_forward, (buffer, gate_w, up_w, down_w))
    fwd_out = collect(blocks, weighing, result_list)
    grad_blocks, grad_weighing, grad_buffer = dispatch(cotangent, b_routes, b_probs)
    grads = lax.map(expert_backward, (grad_buffer, stored, gate_w, up_w, down_w))
    bwd_out = collect(grad_blocks, grad_weighing, grads)
    return fwd_out, bwd_out


def reference(fwd_sent, fwd_routes, fwd_probs, backward_cotangent, bwd_routes, bwd_probs, saved_pre, w_gate, w_up, w_down):
    x_in = jnp.roll(fwd_sent, 1, axis=0)
    fwd_next, bwd_next = lax.map(section_pass, (x_in, fwd_routes, fwd_probs, backward_cotangent, bwd_routes, bwd_probs, saved_pre, w_gate, w_up, w_down))
    experts_iota = jnp.arange(EXP, dtype=jnp.int32)
    counts = jnp.sum((fwd_routes[..., None] == experts_iota).astype(jnp.int32), axis=(1, 2))
    counts = counts + jnp.sum((bwd_routes[..., None] == experts_iota).astype(jnp.int32), axis=(1, 2))
    expert_load = jnp.repeat(counts, SHARD_GROUP, axis=1)
    return fwd_next, bwd_next, expert_load.astype(jnp.int32)
```

```python
import functools

import jax
import jax.numpy as jnp
from jax import lax
from jax.experimental import pallas as pl
from jax.experimental.pallas import tpu as pltpu
from jax.sharding import PartitionSpec as P

MESH = pl.DeviceIdType.MESH
LEFT, RIGHT = 0, 1
FWD, BWD = 0, 1
GATHER_CHUNKS = 2
RETURN_CHUNKS = 2


def from_behind(array, axis, by):
    length = lax.axis_size(axis)
    return lax.ppermute(array, axis, [(i, (i + by) % length) for i in range(length)])


def slot_tables(routes, probs, exp_count, capacity):
    slot_count = exp_count * capacity
    flat_routes = routes.reshape(-1)
    onehot = (flat_routes[:, None] == jnp.arange(exp_count, dtype=jnp.int32)[None, :]).astype(
        jnp.int32
    )
    before = jnp.cumsum(onehot, axis=0) - onehot
    position = jnp.sum(before * onehot, axis=1)
    slot_ids = flat_routes * capacity + position
    matches = (slot_ids[:, None] == jnp.arange(slot_count, dtype=jnp.int32)[None, :]).astype(
        jnp.float32
    )
    matches = matches.reshape(routes.shape[0], routes.shape[1], slot_count)
    placing = jnp.sum(matches, axis=1)
    weighing = jnp.sum(matches * probs[:, :, None], axis=1)
    counted = jnp.sum(onehot, axis=0)
    return (placing, weighing, counted)


def cuts(width, wanted):
    count = max(c for c in range(1, wanted + 1) if width % (c * 128) == 0)
    step = width // count
    return [pl.ds(i * step, step) for i in range(count)]


def relay_kernel(
    size,
    x_ref,
    cot_ref,
    f_routes,
    b_routes,
    f_probs,
    b_probs,
    saved_hbm,
    gate_hbm,
    up_hbm,
    down_hbm,
    f_out,
    b_out,
    load_out,
    gate_w,
    up_w,
    down_w,
    saved,
    rows_all,
    meta,
    from_right,
    from_left,
    going,
    part,
    hidden_acc,
    mid,
    w_sem,
    shift_send,
    shift_recv,
    meta_send,
    meta_recv,
    g_send,
    g_recv,
    r_send,
    r_recv,
):
    n, n_dp, n_sec, sharing, cap, rows = size
    group = n * n_dp
    width = cot_ref.shape[1]
    me = lax.axis_index("expert")
    dp = lax.axis_index("dp")
    sec = lax.axis_index("section")
    lin = me * n_dp + dp
    g_cuts = cuts(width, GATHER_CHUNKS)
    r_cuts = cuts(width, RETURN_CHUNKS)
    contract_last = (((1,), (1,)), ((), ()))

    loads = [
        pltpu.make_async_copy(down_hbm, down_w, w_sem.at[0]),
        pltpu.make_async_copy(saved_hbm, saved, w_sem.at[1]),
        pltpu.make_async_copy(gate_hbm, gate_w, w_sem.at[2]),
        pltpu.make_async_copy(up_hbm, up_w, w_sem.at[3]),
    ]
    for load in loads:
        load.start()

    def place(block):
        return pl.ds(pl.multiple_of(block * rows, rows), rows)

    barrier = pltpu.get_barrier_semaphore()

    def peer(off):
        other = lax.rem(lin + off, group)
        return {"expert": lax.div(other, n_dp), "dp": lax.rem(other, n_dp)}

    for off in range(1, group):
        pl.semaphore_signal(barrier, inc=1, device_id=peer(off), device_id_type=MESH)
    pl.semaphore_signal(
        barrier,
        inc=1,
        device_id={"section": lax.rem(sec + n_sec - 1, n_sec)},
        device_id_type=MESH,
    )

    at_row = lax.broadcasted_iota(jnp.int32, (rows, rows), 0)
    at_col = lax.broadcasted_iota(jnp.int32, (rows, rows), 1)
    eye = at_row == at_col
    meta[lin] = jnp.zeros(meta.shape[1:], jnp.float32)
    for span, routes in ((FWD, f_routes), (BWD, b_routes)):
        named = jnp.broadcast_to(routes[...].astype(jnp.float32), (rows, rows))
        named_row = jnp.sum(jnp.where(eye, named, 0.0), axis=0, keepdims=True)
        earlier = jnp.where((named == named_row) & (at_row < at_col), 1.0, 0.0)
        slot = named_row * cap + jnp.sum(earlier, axis=0, keepdims=True)
        meta[lin, span : span + 1, 0:rows] = slot
    rows_all[BWD, place(me), :] = cot_ref[...]

    pl.semaphore_wait(barrier, group)

    def gather_copy(span, way, hop, chunk):
        block = me - (hop - 1) if way == RIGHT else me + (hop - 1)
        there = me + 1 if way == RIGHT else me - 1
        piece = rows_all.at[span, place(block), g_cuts[chunk]]
        return pltpu.make_async_remote_copy(
            src_ref=piece,
            dst_ref=piece,
            send_sem=g_send.at[span, way, hop - 1, chunk],
            recv_sem=g_recv.at[span, way, hop - 1, chunk],
            device_id={"expert": there},
            device_id_type=MESH,
        )

    def gather_sends(way, hop):
        if way == RIGHT:
            return (me >= hop - 1) & (me < n - 1)
        return (me <= n - hop) & (me > 0)

    def gather_wait(span, way, hop, chunk):
        block = me - hop if way == RIGHT else me + hop
        there = me - 1 if way == RIGHT else me + 1
        piece = rows_all.at[span, place(block), g_cuts[chunk]]
        pltpu.make_async_remote_copy(
            src_ref=piece,
            dst_ref=piece,
            send_sem=g_send.at[span, way, hop - 1, chunk],
            recv_sem=g_recv.at[span, way, hop - 1, chunk],
            device_id={"expert": there},
            device_id_type=MESH,
        ).wait_recv()

    def gather_start(span, hop):
        for chunk in range(len(g_cuts)):
            for way in (LEFT, RIGHT):

                @pl.when(gather_sends(way, hop))
                def _():
                    gather_copy(span, way, hop, chunk).start()

    def gather_step(span, hop, chunk):
        for way in (LEFT, RIGHT):
            there = me >= hop if way == RIGHT else me + hop < n

            @pl.when(there)
            def _():
                gather_wait(span, way, hop, chunk)

            if hop < n - 1:

                @pl.when(gather_sends(way, hop + 1))
                def _():
                    gather_copy(span, way, hop + 1, chunk).start()

    def return_copy(span, way, block, chunk):
        landing = from_left if way == RIGHT else from_right
        there = me + 1 if way == RIGHT else me - 1
        spot = pl.ds(block * rows, rows)
        return pltpu.make_async_remote_copy(
            src_ref=going.at[span, spot, r_cuts[chunk]],
            dst_ref=landing.at[span, spot, r_cuts[chunk]],
            send_sem=r_send.at[span, way, block, chunk],
            recv_sem=r_recv.at[span, way, block, chunk],
            device_id={"expert": there},
            device_id_type=MESH,
        )

    def return_wait(span, way, block, chunk):
        landing = from_left if way == RIGHT else from_right
        there = me - 1 if way == RIGHT else me + 1
        piece = landing.at[span, place(block), r_cuts[chunk]]
        pltpu.make_async_remote_copy(
            src_ref=piece,
            dst_ref=piece,
            send_sem=r_send.at[span, way, block, chunk],
            recv_sem=r_recv.at[span, way, block, chunk],
            device_id={"expert": there},
            device_id_type=MESH,
        ).wait_recv()

    def return_step(span, hop, chunk):
        for way in (LEFT, RIGHT):
            at = n - 1 - hop if way == LEFT else hop
            blocks = range(at) if way == LEFT else range(n - 1, at, -1)
            landing = from_left if way == RIGHT else from_right

            @pl.when(me == at)
            def _():
                for block in blocks:
                    spot = pl.ds(block * rows, rows)
                    total = part[span, spot, r_cuts[chunk]]
                    if hop > 0:
                        return_wait(span, way, block, chunk)
                        total = total + landing[span, spot, r_cuts[chunk]].astype(jnp.float32)
                    going[span, spot, r_cuts[chunk]] = total.astype(jnp.bfloat16)
                    return_copy(span, way, block, chunk).start()

    def finish(span, chunk, base, probs, out):
        spot = place(me)
        for way in (LEFT, RIGHT):
            landing = from_left if way == RIGHT else from_right
            there = me > 0 if way == RIGHT else me < n - 1

            @pl.when(there)
            def _():
                return_wait(span, way, me, chunk)
                part[span, spot, r_cuts[chunk]] += landing[span, spot, r_cuts[chunk]].astype(
                    jnp.float32
                )

        out[:, r_cuts[chunk]] = (
            base(r_cuts[chunk]).astype(jnp.float32) + probs[...] * part[span, spot, r_cuts[chunk]]
        ).astype(jnp.bfloat16)

    def meta_copy(off):
        return pltpu.make_async_remote_copy(
            src_ref=meta.at[lin],
            dst_ref=meta.at[lin],
            send_sem=meta_send.at[off],
            recv_sem=meta_recv.at[off],
            device_id=peer(off),
            device_id_type=MESH,
        )

    def meta_wait(off):
        other = meta.at[lax.rem(lin + group - off, group)]
        pltpu.make_async_remote_copy(
            src_ref=other,
            dst_ref=other,
            send_sem=meta_send.at[off],
            recv_sem=meta_recv.at[off],
            device_id=peer(group - off),
            device_id_type=MESH,
        ).wait_recv()

    shift = pltpu.make_async_remote_copy(
        src_ref=x_ref,
        dst_ref=rows_all.at[FWD, place(me), :],
        send_sem=shift_send,
        recv_sem=shift_recv,
        device_id={"section": lax.rem(sec + 1, n_sec)},
        device_id_type=MESH,
    )

    gather_start(BWD, 1)
    shift.start()
    for off in range(1, group):
        meta_copy(off).start()

    for hop in range(1, n - 1):
        for chunk in range(len(g_cuts)):
            gather_step(BWD, hop, chunk)
        if hop == 1:
            for off in range(1, group):
                meta_wait(off)
            first = (lax.div(me, sharing) * cap).astype(jnp.float32)
            owned = jnp.zeros((2, rows), jnp.float32)
            for other in range(group):
                slots = meta[other, 0:2, 0:rows] - first
                owned = owned + jnp.where((slots >= 0.0) & (slots < cap), 1.0, 0.0)
            owned = jnp.sum(jnp.sum(owned, axis=1, keepdims=True), axis=0, keepdims=True)
            load_out[...] = owned.astype(jnp.int32)

            def slots_of(span, block):
                line = meta[block * n_dp + dp, span : span + 1, 0:rows] - first
                spread = jnp.where(eye, jnp.broadcast_to(line, (rows, rows)), 0.0)
                return jnp.sum(spread, axis=1, keepdims=True)

            lanes = lax.broadcasted_iota(jnp.int32, (rows, n * cap), 1).astype(jnp.float32)
            taken = []
            for block in range(n):
                slots = slots_of(BWD, block)
                hit = (slots >= 0.0) & (slots < cap) & (lanes == slots + block * cap)
                taken.append(jnp.where(hit, 1.0, 0.0))
            taken = jnp.concatenate(taken, axis=0).astype(jnp.bfloat16)
            kept = []
            for block in range(n):
                slots = slots_of(FWD, block)
                kept.append(jnp.where((slots >= 0.0) & (slots < cap), 1.0, 0.0))
            kept = jnp.concatenate(kept, axis=0) > 0.5
            loads[1].wait()
            stored = saved[...].astype(jnp.float32)
            saved_gate = jnp.dot(
                taken, stored[:, 0, :].astype(jnp.bfloat16), preferred_element_type=jnp.float32
            )
            saved_up = jnp.dot(
                taken, stored[:, 1, :].astype(jnp.bfloat16), preferred_element_type=jnp.float32
            )
            sigma = jax.nn.sigmoid(saved_gate)
            hidden_acc[0] = saved_up * sigma * (1.0 + saved_gate * (1.0 - sigma))
            hidden_acc[1] = saved_gate * sigma

    shift.wait_recv()
    gather_start(FWD, 1)
    loads[0].wait()
    for chunk, cut in enumerate(g_cuts):
        gather_step(BWD, n - 1, chunk)
        term = lax.dot_general(
            rows_all[BWD, :, cut],
            down_w[:, cut],
            contract_last,
            preferred_element_type=jnp.float32,
        )
        if chunk == 0:
            hidden_acc[2] = term
        else:
            hidden_acc[2] += term
    mid[0] = (hidden_acc[2] * hidden_acc[0]).astype(jnp.bfloat16)
    mid[1] = (hidden_acc[2] * hidden_acc[1]).astype(jnp.bfloat16)

    loads[2].wait()
    loads[3].wait()

    def bwd_part(chunk):
        cut = r_cuts[chunk]
        part[BWD, :, cut] = lax.dot_general(
            mid[0], gate_w[cut, :], contract_last, preferred_element_type=jnp.float32
        ) + lax.dot_general(
            mid[1], up_w[cut, :], contract_last, preferred_element_type=jnp.float32
        )

    r_count = len(r_cuts)
    for chunk in range(r_count):
        bwd_part(chunk)
        return_step(BWD, 0, chunk)
        if chunk == 0:
            for piece in range(len(g_cuts)):
                gather_step(FWD, 1, piece)
    for hop in range(1, n - 1):
        for chunk in range(r_count):
            return_step(BWD, hop, chunk)
        if hop + 1 < n - 1:
            for piece in range(len(g_cuts)):
                gather_step(FWD, hop + 1, piece)

    for chunk, cut in enumerate(g_cuts):
        if n > 2:
            gather_step(FWD, n - 1, chunk)
        for at, weights in ((0, gate_w), (1, up_w)):
            term = jnp.dot(
                rows_all[FWD, :, cut], weights[cut, :], preferred_element_type=jnp.float32
            )
            if chunk == 0:
                hidden_acc[at] = term
            else:
                hidden_acc[at] += term
    activated = jax.nn.silu(hidden_acc[0]) * hidden_acc[1]
    mid[0] = jnp.where(kept, activated, 0.0).astype(jnp.bfloat16)

    for chunk in range(r_count):
        cut = r_cuts[chunk]
        part[FWD, :, cut] = jnp.dot(mid[0], down_w[:, cut], preferred_element_type=jnp.float32)
        return_step(FWD, 0, chunk)
    for chunk in range(r_count):
        finish(BWD, chunk, lambda cut: cot_ref[:, cut], b_probs, b_out)
    for hop in range(1, n - 1):
        for chunk in range(r_count):
            return_step(FWD, hop, chunk)
    for chunk in range(r_count):
        finish(FWD, chunk, lambda cut: rows_all[FWD, place(me), cut], f_probs, f_out)

    shift.wait_send()
    for off in range(1, group):
        meta_copy(off).wait_send()
    for span in (BWD, FWD):
        for way in (LEFT, RIGHT):
            for hop in range(1, n):

                @pl.when(gather_sends(way, hop))
                def _():
                    for chunk in range(len(g_cuts)):
                        gather_copy(span, way, hop, chunk).wait_send()

            for block in range(n):

                @pl.when(me > block if way == LEFT else me < block)
                def _():
                    for chunk in range(r_count):
                        return_copy(span, way, block, chunk).wait_send()


def relay_fits(fwd_sent, top_count, capacity):
    rows, width = fwd_sent.shape[1:]
    return (
        top_count == 1
        and capacity == rows
        and rows % 16 == 0
        and rows <= 128
        and width % 256 == 0
        and lax.axis_size("expert") > 2
        and lax.axis_size("section") > 1
    )


def relay(
    fwd_sent,
    fwd_routes,
    fwd_probs,
    backward_cotangent,
    bwd_routes,
    bwd_probs,
    saved_pre,
    w_gate,
    w_up,
    w_down,
    *,
    sharing,
    capacity,
):
    n, n_dp, n_sec = (lax.axis_size(name) for name in ("expert", "dp", "section"))
    rows, width = fwd_sent.shape[1:]
    hidden = w_gate.shape[2]
    tokens = n * rows
    bf16, f32 = jnp.bfloat16, jnp.float32
    group = n * n_dp
    g_count = len(cuts(width, GATHER_CHUNKS))
    r_count = len(cuts(width, RETURN_CHUNKS))
    vmem = pl.BlockSpec(memory_space=pltpu.VMEM)
    hbm = pl.BlockSpec(memory_space=pl.ANY)
    f_next, b_next, load = pl.pallas_call(
        functools.partial(relay_kernel, (n, n_dp, n_sec, sharing, capacity, rows)),
        out_shape=(
            jax.ShapeDtypeStruct((rows, width), bf16),
            jax.ShapeDtypeStruct((rows, width), bf16),
            jax.ShapeDtypeStruct((1, 1), jnp.int32),
        ),
        in_specs=[vmem] * 6 + [hbm] * 4,
        out_specs=(vmem, vmem, vmem),
        scratch_shapes=[
            pltpu.VMEM((width, hidden), bf16),
            pltpu.VMEM((width, hidden), bf16),
            pltpu.VMEM((hidden, width), bf16),
            pltpu.VMEM(saved_pre.shape[2:], bf16),
            pltpu.VMEM((2, tokens, width), bf16),
            pltpu.VMEM((group, 8, 128), f32),
            pltpu.VMEM((2, tokens, width), bf16),
            pltpu.VMEM((2, tokens, width), bf16),
            pltpu.VMEM((2, tokens, width), bf16),
            pltpu.VMEM((2, tokens, width), f32),
            pltpu.VMEM((3, tokens, hidden), f32),
            pltpu.VMEM((2, tokens, hidden), bf16),
            pltpu.SemaphoreType.DMA((4,)),
            pltpu.SemaphoreType.DMA,
            pltpu.SemaphoreType.DMA,
            pltpu.SemaphoreType.DMA((group,)),
            pltpu.SemaphoreType.DMA((group,)),
            pltpu.SemaphoreType.DMA((2, 2, n - 1, g_count)),
            pltpu.SemaphoreType.DMA((2, 2, n - 1, g_count)),
            pltpu.SemaphoreType.DMA((2, 2, n, r_count)),
            pltpu.SemaphoreType.DMA((2, 2, n, r_count)),
        ],
        compiler_params=pltpu.CompilerParams(
            collective_id=0, has_side_effects=True, vmem_limit_bytes=48 * 1024 * 1024
        ),
        cost_estimate=pl.CostEstimate(
            flops=12 * tokens * width * hidden,
            bytes_accessed=6 * width * hidden,
            transcendentals=2 * tokens * hidden,
        ),
    )(
        fwd_sent[0],
        backward_cotangent[0],
        fwd_routes[0],
        bwd_routes[0],
        fwd_probs[0],
        bwd_probs[0],
        saved_pre[0, 0],
        w_gate[0],
        w_up[0],
        w_down[0],
    )
    return f_next[None], b_next[None], load


def shards(
    fwd_sent,
    fwd_routes,
    fwd_probs,
    backward_cotangent,
    bwd_routes,
    bwd_probs,
    saved_pre,
    w_gate,
    w_up,
    w_down,
):
    experts = lax.axis_size("expert")
    sharing = min(4, experts // 2)
    exp_count = experts // sharing
    token_rows = fwd_sent.shape[1]
    top_count = fwd_routes.shape[2]
    capacity = min(token_rows, max(2, 2 * token_rows * top_count // exp_count))
    slot_count = experts * capacity
    if relay_fits(fwd_sent, top_count, capacity):
        return relay(
            fwd_sent,
            fwd_routes,
            fwd_probs,
            backward_cotangent,
            bwd_routes,
            bwd_probs,
            saved_pre,
            w_gate,
            w_up,
            w_down,
            sharing=sharing,
            capacity=capacity,
        )
    arrived = from_behind(fwd_sent, "section", 1)[0]
    gate_mat = w_gate[0]
    up_mat = w_up[0]
    down_mat = w_down[0]
    stored = saved_pre[0, 0]
    cotangent = backward_cotangent[0]
    fwd_place, fwd_weigh, fwd_count = slot_tables(fwd_routes[0], fwd_probs[0], exp_count, capacity)
    bwd_place, bwd_weigh, bwd_count = slot_tables(bwd_routes[0], bwd_probs[0], exp_count, capacity)

    def forward_rows(slot_rows):
        gate_pre = jnp.dot(slot_rows, gate_mat, preferred_element_type=jnp.float32)
        up_pre = jnp.dot(slot_rows, up_mat, preferred_element_type=jnp.float32)
        hidden_state = (jax.nn.silu(gate_pre) * up_pre).astype(jnp.bfloat16)
        return jnp.dot(hidden_state, down_mat, preferred_element_type=jnp.float32).astype(
            jnp.bfloat16
        )

    def backward_rows(slot_rows):
        contract = (((1,), (1,)), ((), ()))
        grad_hidden = lax.dot_general(
            slot_rows, down_mat, contract, preferred_element_type=jnp.float32
        )
        saved_gate = stored[:, 0].astype(jnp.float32)
        saved_up = stored[:, 1].astype(jnp.float32)
        sigma = jax.nn.sigmoid(saved_gate)
        grad_gate = (grad_hidden * saved_up * sigma * (1.0 + saved_gate * (1.0 - sigma))).astype(
            jnp.bfloat16
        )
        grad_up = (grad_hidden * saved_gate * sigma).astype(jnp.bfloat16)
        summed = lax.dot_general(grad_gate, gate_mat, contract, preferred_element_type=jnp.float32)
        summed = summed + lax.dot_general(
            grad_up, up_mat, contract, preferred_element_type=jnp.float32
        )
        return summed.astype(jnp.bfloat16)

    def send_rows(tokens, placing):
        width = tokens.shape[1]
        outgoing = jnp.dot(
            placing.T.astype(jnp.bfloat16), tokens, preferred_element_type=jnp.float32
        )
        outgoing = outgoing.astype(jnp.bfloat16).reshape(exp_count, 1, capacity, width)
        outgoing = jnp.broadcast_to(outgoing, (exp_count, sharing, capacity, width)).reshape(
            experts, capacity, width
        )
        received = lax.all_to_all(outgoing, "expert", split_axis=0, concat_axis=0, tiled=True)
        owned = jnp.zeros((), jnp.int32)
        return (received.reshape(slot_count, width), owned)

    def finish_rows(received, compute):
        width = received.shape[1]
        result_list = compute(received)
        returned = lax.all_to_all(
            result_list.reshape(experts, capacity, width),
            "expert",
            split_axis=0,
            concat_axis=0,
            tiled=True,
        )
        gathered = jnp.sum(
            returned.reshape(exp_count, sharing, capacity, width).astype(jnp.float32), axis=1
        )
        return gathered.reshape(exp_count * capacity, width)

    fwd_rows, fwd_owned = send_rows(arrived, fwd_place)
    fwd_back = finish_rows(fwd_rows, forward_rows)
    bwd_rows, bwd_owned = send_rows(cotangent, bwd_place)
    bwd_back = finish_rows(bwd_rows, backward_rows)
    fwd_next = arrived.astype(jnp.float32) + jnp.dot(
        fwd_weigh, fwd_back, precision=lax.Precision.HIGHEST
    )
    bwd_next = cotangent.astype(jnp.float32) + jnp.dot(
        bwd_weigh, bwd_back, precision=lax.Precision.HIGHEST
    )
    totals = lax.psum(fwd_count + bwd_count, ("expert", "dp"))
    expert_load = lax.dynamic_slice_in_dim(totals, lax.axis_index("expert") // sharing, 1)[0]
    return (
        fwd_next.astype(jnp.bfloat16)[None],
        bwd_next.astype(jnp.bfloat16)[None],
        expert_load.reshape(1, 1),
    )


def solution(mesh):
    in_specs = (
        P("section", ("expert", "dp"), None),
        P("section", ("expert", "dp"), None),
        P("section", ("expert", "dp"), None),
        P("section", ("expert", "dp"), None),
        P("section", ("expert", "dp"), None),
        P("section", ("expert", "dp"), None),
        P("section", "dp", None, None, "expert"),
        P("section", None, "expert"),
        P("section", None, "expert"),
        P("section", "expert", None),
    )
    out_specs = (
        P("section", ("expert", "dp"), None),
        P("section", ("expert", "dp"), None),
        P("section", "expert"),
    )
    return jax.shard_map(shards, mesh=mesh, in_specs=in_specs, out_specs=out_specs, check_vma=False)
```

```python
import functools

import jax
import jax.numpy as jnp
from jax import lax
from jax.experimental import pallas as pl
from jax.experimental.pallas import tpu as pltpu
from jax.sharding import PartitionSpec as P

MESH = pl.DeviceIdType.MESH
LEFT, RIGHT = 0, 1
FWD, BWD = 0, 1
GATHER_CHUNKS = 2
RETURN_CHUNKS = 2


def from_behind(array, axis, by):
    length = lax.axis_size(axis)
    return lax.ppermute(array, axis, [(i, (i + by) % length) for i in range(length)])


def slot_tables(routes, probs, exp_count, capacity):
    slot_count = exp_count * capacity
    flat_routes = routes.reshape(-1)
    onehot = (flat_routes[:, None] == jnp.arange(exp_count, dtype=jnp.int32)[None, :]).astype(
        jnp.int32
    )
    before = jnp.cumsum(onehot, axis=0) - onehot
    position = jnp.sum(before * onehot, axis=1)
    slot_ids = flat_routes * capacity + position
    matches = (slot_ids[:, None] == jnp.arange(slot_count, dtype=jnp.int32)[None, :]).astype(
        jnp.float32
    )
    matches = matches.reshape(routes.shape[0], routes.shape[1], slot_count)
    placing = jnp.sum(matches, axis=1)
    weighing = jnp.sum(matches * probs[:, :, None], axis=1)
    counted = jnp.sum(onehot, axis=0)
    return (placing, weighing, counted)


def cuts(width, wanted):
    count = max(c for c in range(1, wanted + 1) if width % (c * 128) == 0)
    step = width // count
    return [pl.ds(i * step, step) for i in range(count)]


def relay_kernel(
    size,
    x_hbm,
    cot_hbm,
    f_routes,
    b_routes,
    f_probs,
    b_probs,
    saved_hbm,
    gate_hbm,
    up_hbm,
    down_hbm,
    f_out,
    b_out,
    load_out,
    gate_w,
    up_w,
    down_w,
    saved,
    x_own,
    rows_all,
    meta,
    from_right,
    from_left,
    going,
    part,
    hidden_acc,
    mid,
    w_sem,
    shift_send,
    shift_recv,
    meta_send,
    meta_recv,
    g_send,
    g_recv,
    r_send,
    r_recv,
):
    n, n_dp, n_sec, sharing, cap, rows = size
    group = n * n_dp
    width = cot_hbm.shape[1]
    me = lax.axis_index("expert")
    dp = lax.axis_index("dp")
    sec = lax.axis_index("section")
    lin = me * n_dp + dp
    g_cuts = cuts(width, GATHER_CHUNKS)
    r_cuts = cuts(width, RETURN_CHUNKS)
    contract_last = (((1,), (1,)), ((), ()))

    def place(block):
        return pl.ds(pl.multiple_of(block * rows, rows), rows)

    own_rows = [
        pltpu.make_async_copy(x_hbm, x_own, w_sem.at[4]),
        pltpu.make_async_copy(cot_hbm, rows_all.at[BWD, place(me), :], w_sem.at[5]),
    ]
    for load in own_rows:
        load.start()
    loads = [
        pltpu.make_async_copy(down_hbm, down_w, w_sem.at[0]),
        pltpu.make_async_copy(saved_hbm, saved, w_sem.at[1]),
        pltpu.make_async_copy(gate_hbm, gate_w, w_sem.at[2]),
        pltpu.make_async_copy(up_hbm, up_w, w_sem.at[3]),
    ]
    for load in loads[:2]:
        load.start()

    barrier = pltpu.get_barrier_semaphore()

    def peer(off):
        other = lax.rem(lin + off, group)
        return {"expert": lax.div(other, n_dp), "dp": lax.rem(other, n_dp)}

    for off in range(1, group):
        pl.semaphore_signal(barrier, inc=1, device_id=peer(off), device_id_type=MESH)
    pl.semaphore_signal(
        barrier,
        inc=1,
        device_id={"section": lax.rem(sec + n_sec - 1, n_sec)},
        device_id_type=MESH,
    )

    at_row = lax.broadcasted_iota(jnp.int32, (rows, rows), 0)
    at_col = lax.broadcasted_iota(jnp.int32, (rows, rows), 1)
    eye = at_row == at_col

    def column(line):
        spread = jnp.where(eye, jnp.broadcast_to(line, (rows, rows)), 0.0)
        return jnp.sum(spread, axis=1, keepdims=True)

    meta[lin] = jnp.zeros(meta.shape[1:], jnp.float32)
    for span, routes in ((FWD, f_routes), (BWD, b_routes)):
        named_row = routes[...].astype(jnp.float32)
        named = column(named_row)
        earlier = jnp.where((named == named_row) & (at_row < at_col), 1.0, 0.0)
        slot = named_row * cap + jnp.sum(earlier, axis=0, keepdims=True)
        meta[lin, span : span + 1, 0:rows] = slot
    pl.semaphore_wait(barrier, group)

    def gather_copy(span, way, hop, chunk):
        block = me - (hop - 1) if way == RIGHT else me + (hop - 1)
        there = me + 1 if way == RIGHT else me - 1
        piece = rows_all.at[span, place(block), g_cuts[chunk]]
        return pltpu.make_async_remote_copy(
            src_ref=piece,
            dst_ref=piece,
            send_sem=g_send.at[span, way, hop - 1, chunk],
            recv_sem=g_recv.at[span, way, hop - 1, chunk],
            device_id={"expert": there},
            device_id_type=MESH,
        )

    def gather_sends(way, hop):
        if way == RIGHT:
            return (me >= hop - 1) & (me < n - 1)
        return (me <= n - hop) & (me > 0)

    def gather_wait(span, way, hop, chunk):
        block = me - hop if way == RIGHT else me + hop
        there = me - 1 if way == RIGHT else me + 1
        piece = rows_all.at[span, place(block), g_cuts[chunk]]
        pltpu.make_async_remote_copy(
            src_ref=piece,
            dst_ref=piece,
            send_sem=g_send.at[span, way, hop - 1, chunk],
            recv_sem=g_recv.at[span, way, hop - 1, chunk],
            device_id={"expert": there},
            device_id_type=MESH,
        ).wait_recv()

    def gather_start(span, hop, chunk):
        for way in (LEFT, RIGHT):

            @pl.when(gather_sends(way, hop))
            def _():
                gather_copy(span, way, hop, chunk).start()

    def gather_step(span, hop, chunk):
        for way in (LEFT, RIGHT):
            there = me >= hop if way == RIGHT else me + hop < n

            @pl.when(there)
            def _():
                gather_wait(span, way, hop, chunk)

            if hop < n - 1:

                @pl.when(gather_sends(way, hop + 1))
                def _():
                    gather_copy(span, way, hop + 1, chunk).start()

    def return_copy(span, way, block, chunk):
        landing = from_left if way == RIGHT else from_right
        there = me + 1 if way == RIGHT else me - 1
        spot = pl.ds(block * rows, rows)
        return pltpu.make_async_remote_copy(
            src_ref=going.at[span, spot, r_cuts[chunk]],
            dst_ref=landing.at[span, spot, r_cuts[chunk]],
            send_sem=r_send.at[span, way, block, chunk],
            recv_sem=r_recv.at[span, way, block, chunk],
            device_id={"expert": there},
            device_id_type=MESH,
        )

    def return_wait(span, way, block, chunk):
        landing = from_left if way == RIGHT else from_right
        there = me - 1 if way == RIGHT else me + 1
        piece = landing.at[span, place(block), r_cuts[chunk]]
        pltpu.make_async_remote_copy(
            src_ref=piece,
            dst_ref=piece,
            send_sem=r_send.at[span, way, block, chunk],
            recv_sem=r_recv.at[span, way, block, chunk],
            device_id={"expert": there},
            device_id_type=MESH,
        ).wait_recv()

    def return_step(span, hop, chunk):
        for way in (LEFT, RIGHT):
            at = n - 1 - hop if way == LEFT else hop
            blocks = range(at) if way == LEFT else range(n - 1, at, -1)
            landing = from_left if way == RIGHT else from_right

            @pl.when(me == at)
            def _():
                for block in blocks:
                    spot = pl.ds(block * rows, rows)
                    total = part[span, spot, r_cuts[chunk]]
                    if hop > 0:
                        return_wait(span, way, block, chunk)
                        total = total + landing[span, spot, r_cuts[chunk]].astype(jnp.float32)
                    going[span, spot, r_cuts[chunk]] = total.astype(jnp.bfloat16)
                    return_copy(span, way, block, chunk).start()

    def finish(span, chunk, base, probs, out):
        spot = place(me)
        for way in (LEFT, RIGHT):
            landing = from_left if way == RIGHT else from_right
            there = me > 0 if way == RIGHT else me < n - 1

            @pl.when(there)
            def _():
                return_wait(span, way, me, chunk)
                part[span, spot, r_cuts[chunk]] += landing[span, spot, r_cuts[chunk]].astype(
                    jnp.float32
                )

        out[:, r_cuts[chunk]] = (
            base(r_cuts[chunk]).astype(jnp.float32) + column(probs[...]) * part[span, spot, r_cuts[chunk]]
        ).astype(jnp.bfloat16)

    def meta_copy(off):
        return pltpu.make_async_remote_copy(
            src_ref=meta.at[lin],
            dst_ref=meta.at[lin],
            send_sem=meta_send.at[off],
            recv_sem=meta_recv.at[off],
            device_id=peer(off),
            device_id_type=MESH,
        )

    def meta_wait(off):
        other = meta.at[lax.rem(lin + group - off, group)]
        pltpu.make_async_remote_copy(
            src_ref=other,
            dst_ref=other,
            send_sem=meta_send.at[off],
            recv_sem=meta_recv.at[off],
            device_id=peer(group - off),
            device_id_type=MESH,
        ).wait_recv()

    def shift_copy(chunk):
        return pltpu.make_async_remote_copy(
            src_ref=x_own.at[:, g_cuts[chunk]],
            dst_ref=rows_all.at[FWD, place(me), g_cuts[chunk]],
            send_sem=shift_send.at[chunk],
            recv_sem=shift_recv.at[chunk],
            device_id={"section": lax.rem(sec + 1, n_sec)},
            device_id_type=MESH,
        )

    own_rows[0].wait()
    for chunk in range(len(g_cuts)):
        shift_copy(chunk).start()
    own_rows[1].wait()
    for chunk in range(len(g_cuts)):
        gather_start(BWD, 1, chunk)
    for load in loads[2:]:
        load.start()
    for off in range(1, group):
        meta_copy(off).start()

    for hop in range(1, n - 1):
        for chunk in range(len(g_cuts)):
            gather_step(BWD, hop, chunk)
        if hop == 1:
            for off in range(1, group):
                meta_wait(off)
            first = (lax.div(me, sharing) * cap).astype(jnp.float32)
            owned = jnp.zeros((2, rows), jnp.float32)
            for other in range(group):
                slots = meta[other, 0:2, 0:rows] - first
                owned = owned + jnp.where((slots >= 0.0) & (slots < cap), 1.0, 0.0)
            owned = jnp.sum(jnp.sum(owned, axis=1, keepdims=True), axis=0, keepdims=True)
            load_out[...] = owned.astype(jnp.int32)

            def slots_of(span, block):
                line = meta[block * n_dp + dp, span : span + 1, 0:rows] - first
                return column(line)

            lanes = lax.broadcasted_iota(jnp.int32, (rows, n * cap), 1).astype(jnp.float32)
            taken = []
            for block in range(n):
                slots = slots_of(BWD, block)
                hit = (slots >= 0.0) & (slots < cap) & (lanes == slots + block * cap)
                taken.append(jnp.where(hit, 1.0, 0.0))
            taken = jnp.concatenate(taken, axis=0).astype(jnp.bfloat16)
            kept = []
            for block in range(n):
                slots = slots_of(FWD, block)
                kept.append(jnp.where((slots >= 0.0) & (slots < cap), 1.0, 0.0))
            kept = jnp.concatenate(kept, axis=0) > 0.5
            loads[1].wait()
            stored = saved[...].astype(jnp.float32)
            saved_gate = jnp.dot(
                taken, stored[:, 0, :].astype(jnp.bfloat16), preferred_element_type=jnp.float32
            )
            saved_up = jnp.dot(
                taken, stored[:, 1, :].astype(jnp.bfloat16), preferred_element_type=jnp.float32
            )
            sigma = jax.nn.sigmoid(saved_gate)
            hidden_acc[0] = saved_up * sigma * (1.0 + saved_gate * (1.0 - sigma))
            hidden_acc[1] = saved_gate * sigma

    for chunk in range(len(g_cuts)):
        shift_copy(chunk).wait_recv()
        gather_start(FWD, 1, chunk)
    loads[0].wait()
    for chunk, cut in enumerate(g_cuts):
        gather_step(BWD, n - 1, chunk)
        term = lax.dot_general(
            rows_all[BWD, :, cut],
            down_w[:, cut],
            contract_last,
            preferred_element_type=jnp.float32,
        )
        if chunk == 0:
            hidden_acc[2] = term
        else:
            hidden_acc[2] += term
    mid[0] = (hidden_acc[2] * hidden_acc[0]).astype(jnp.bfloat16)
    mid[1] = (hidden_acc[2] * hidden_acc[1]).astype(jnp.bfloat16)

    loads[2].wait()
    loads[3].wait()

    def bwd_part(chunk):
        cut = r_cuts[chunk]
        part[BWD, :, cut] = lax.dot_general(
            mid[0], gate_w[cut, :], contract_last, preferred_element_type=jnp.float32
        ) + lax.dot_general(
            mid[1], up_w[cut, :], contract_last, preferred_element_type=jnp.float32
        )

    r_count = len(r_cuts)
    for chunk in range(r_count):
        bwd_part(chunk)
        return_step(BWD, 0, chunk)
        if chunk == 0:
            for piece in range(len(g_cuts)):
                gather_step(FWD, 1, piece)
    for hop in range(1, n - 1):
        for chunk in range(r_count):
            return_step(BWD, hop, chunk)
        if hop + 1 < n - 1:
            for piece in range(len(g_cuts)):
                gather_step(FWD, hop + 1, piece)

    for chunk, cut in enumerate(g_cuts):
        if n > 2:
            gather_step(FWD, n - 1, chunk)
        for at, weights in ((0, gate_w), (1, up_w)):
            term = jnp.dot(
                rows_all[FWD, :, cut], weights[cut, :], preferred_element_type=jnp.float32
            )
            if chunk == 0:
                hidden_acc[at] = term
            else:
                hidden_acc[at] += term
    activated = jax.nn.silu(hidden_acc[0]) * hidden_acc[1]
    mid[0] = jnp.where(kept, activated, 0.0).astype(jnp.bfloat16)

    for chunk in range(r_count):
        cut = r_cuts[chunk]
        part[FWD, :, cut] = jnp.dot(mid[0], down_w[:, cut], preferred_element_type=jnp.float32)
        return_step(FWD, 0, chunk)
    for chunk in range(r_count):
        finish(BWD, chunk, lambda cut: rows_all[BWD, place(me), cut], b_probs, b_out)
    for hop in range(1, n - 1):
        for chunk in range(r_count):
            return_step(FWD, hop, chunk)
    for chunk in range(r_count):
        finish(FWD, chunk, lambda cut: rows_all[FWD, place(me), cut], f_probs, f_out)

    for chunk in range(len(g_cuts)):
        shift_copy(chunk).wait_send()
    for off in range(1, group):
        meta_copy(off).wait_send()
    for span in (BWD, FWD):
        for way in (LEFT, RIGHT):
            for hop in range(1, n):

                @pl.when(gather_sends(way, hop))
                def _():
                    for chunk in range(len(g_cuts)):
                        gather_copy(span, way, hop, chunk).wait_send()

            for block in range(n):

                @pl.when(me > block if way == LEFT else me < block)
                def _():
                    for chunk in range(r_count):
                        return_copy(span, way, block, chunk).wait_send()


def relay_fits(fwd_sent, top_count, capacity):
    rows, width = fwd_sent.shape[1:]
    return (
        top_count == 1
        and capacity == rows
        and rows % 16 == 0
        and rows <= 128
        and width % 256 == 0
        and lax.axis_size("expert") > 2
        and lax.axis_size("section") > 1
    )


def relay(
    fwd_sent,
    fwd_routes,
    fwd_probs,
    backward_cotangent,
    bwd_routes,
    bwd_probs,
    saved_pre,
    w_gate,
    w_up,
    w_down,
    *,
    sharing,
    capacity,
):
    n, n_dp, n_sec = (lax.axis_size(name) for name in ("expert", "dp", "section"))
    rows, width = fwd_sent.shape[1:]
    hidden = w_gate.shape[2]
    tokens = n * rows
    bf16, f32 = jnp.bfloat16, jnp.float32
    group = n * n_dp
    g_count = len(cuts(width, GATHER_CHUNKS))
    r_count = len(cuts(width, RETURN_CHUNKS))
    vmem = pl.BlockSpec(memory_space=pltpu.VMEM)
    hbm = pl.BlockSpec(memory_space=pl.ANY)
    f_next, b_next, load = pl.pallas_call(
        functools.partial(relay_kernel, (n, n_dp, n_sec, sharing, capacity, rows)),
        out_shape=(
            jax.ShapeDtypeStruct((rows, width), bf16),
            jax.ShapeDtypeStruct((rows, width), bf16),
            jax.ShapeDtypeStruct((1, 1), jnp.int32),
        ),
        in_specs=[hbm] * 2 + [vmem] * 4 + [hbm] * 4,
        out_specs=(vmem, vmem, vmem),
        scratch_shapes=[
            pltpu.VMEM((width, hidden), bf16),
            pltpu.VMEM((width, hidden), bf16),
            pltpu.VMEM((hidden, width), bf16),
            pltpu.VMEM(saved_pre.shape[2:], bf16),
            pltpu.VMEM((rows, width), bf16),
            pltpu.VMEM((2, tokens, width), bf16),
            pltpu.VMEM((group, 8, 128), f32),
            pltpu.VMEM((2, tokens, width), bf16),
            pltpu.VMEM((2, tokens, width), bf16),
            pltpu.VMEM((2, tokens, width), bf16),
            pltpu.VMEM((2, tokens, width), f32),
            pltpu.VMEM((3, tokens, hidden), f32),
            pltpu.VMEM((2, tokens, hidden), bf16),
            pltpu.SemaphoreType.DMA((6,)),
            pltpu.SemaphoreType.DMA((g_count,)),
            pltpu.SemaphoreType.DMA((g_count,)),
            pltpu.SemaphoreType.DMA((group,)),
            pltpu.SemaphoreType.DMA((group,)),
            pltpu.SemaphoreType.DMA((2, 2, n - 1, g_count)),
            pltpu.SemaphoreType.DMA((2, 2, n - 1, g_count)),
            pltpu.SemaphoreType.DMA((2, 2, n, r_count)),
            pltpu.SemaphoreType.DMA((2, 2, n, r_count)),
        ],
        compiler_params=pltpu.CompilerParams(
            collective_id=0, has_side_effects=True, vmem_limit_bytes=60 * 1024 * 1024
        ),
        cost_estimate=pl.CostEstimate(
            flops=12 * tokens * width * hidden,
            bytes_accessed=6 * width * hidden,
            transcendentals=2 * tokens * hidden,
        ),
    )(
        fwd_sent[0],
        backward_cotangent[0],
        fwd_routes.reshape(1, rows),
        bwd_routes.reshape(1, rows),
        fwd_probs.reshape(1, rows),
        bwd_probs.reshape(1, rows),
        saved_pre[0, 0],
        w_gate[0],
        w_up[0],
        w_down[0],
    )
    return f_next[None], b_next[None], load


def shards(
    fwd_sent,
    fwd_routes,
    fwd_probs,
    backward_cotangent,
    bwd_routes,
    bwd_probs,
    saved_pre,
    w_gate,
    w_up,
    w_down,
):
    experts = lax.axis_size("expert")
    sharing = min(4, experts // 2)
    exp_count = experts // sharing
    token_rows = fwd_sent.shape[1]
    top_count = fwd_routes.shape[2]
    capacity = min(token_rows, max(2, 2 * token_rows * top_count // exp_count))
    slot_count = experts * capacity
    if relay_fits(fwd_sent, top_count, capacity):
        return relay(
            fwd_sent,
            fwd_routes,
            fwd_probs,
            backward_cotangent,
            bwd_routes,
            bwd_probs,
            saved_pre,
            w_gate,
            w_up,
            w_down,
            sharing=sharing,
            capacity=capacity,
        )
    arrived = from_behind(fwd_sent, "section", 1)[0]
    gate_mat = w_gate[0]
    up_mat = w_up[0]
    down_mat = w_down[0]
    stored = saved_pre[0, 0]
    cotangent = backward_cotangent[0]
    fwd_place, fwd_weigh, fwd_count = slot_tables(fwd_routes[0], fwd_probs[0], exp_count, capacity)
    bwd_place, bwd_weigh, bwd_count = slot_tables(bwd_routes[0], bwd_probs[0], exp_count, capacity)

    def forward_rows(slot_rows):
        gate_pre = jnp.dot(slot_rows, gate_mat, preferred_element_type=jnp.float32)
        up_pre = jnp.dot(slot_rows, up_mat, preferred_element_type=jnp.float32)
        hidden_state = (jax.nn.silu(gate_pre) * up_pre).astype(jnp.bfloat16)
        return jnp.dot(hidden_state, down_mat, preferred_element_type=jnp.float32).astype(
            jnp.bfloat16
        )

    def backward_rows(slot_rows):
        contract = (((1,), (1,)), ((), ()))
        grad_hidden = lax.dot_general(
            slot_rows, down_mat, contract, preferred_element_type=jnp.float32
        )
        saved_gate = stored[:, 0].astype(jnp.float32)
        saved_up = stored[:, 1].astype(jnp.float32)
        sigma = jax.nn.sigmoid(saved_gate)
        grad_gate = (grad_hidden * saved_up * sigma * (1.0 + saved_gate * (1.0 - sigma))).astype(
            jnp.bfloat16
        )
        grad_up = (grad_hidden * saved_gate * sigma).astype(jnp.bfloat16)
        summed = lax.dot_general(grad_gate, gate_mat, contract, preferred_element_type=jnp.float32)
        summed = summed + lax.dot_general(
            grad_up, up_mat, contract, preferred_element_type=jnp.float32
        )
        return summed.astype(jnp.bfloat16)

    def send_rows(tokens, placing):
        width = tokens.shape[1]
        outgoing = jnp.dot(
            placing.T.astype(jnp.bfloat16), tokens, preferred_element_type=jnp.float32
        )
        outgoing = outgoing.astype(jnp.bfloat16).reshape(exp_count, 1, capacity, width)
        outgoing = jnp.broadcast_to(outgoing, (exp_count, sharing, capacity, width)).reshape(
            experts, capacity, width
        )
        received = lax.all_to_all(outgoing, "expert", split_axis=0, concat_axis=0, tiled=True)
        owned = jnp.zeros((), jnp.int32)
        return (received.reshape(slot_count, width), owned)

    def finish_rows(received, compute):
        width = received.shape[1]
        result_list = compute(received)
        returned = lax.all_to_all(
            result_list.reshape(experts, capacity, width),
            "expert",
            split_axis=0,
            concat_axis=0,
            tiled=True,
        )
        gathered = jnp.sum(
            returned.reshape(exp_count, sharing, capacity, width).astype(jnp.float32), axis=1
        )
        return gathered.reshape(exp_count * capacity, width)

    fwd_rows, fwd_owned = send_rows(arrived, fwd_place)
    fwd_back = finish_rows(fwd_rows, forward_rows)
    bwd_rows, bwd_owned = send_rows(cotangent, bwd_place)
    bwd_back = finish_rows(bwd_rows, backward_rows)
    fwd_next = arrived.astype(jnp.float32) + jnp.dot(
        fwd_weigh, fwd_back, precision=lax.Precision.HIGHEST
    )
    bwd_next = cotangent.astype(jnp.float32) + jnp.dot(
        bwd_weigh, bwd_back, precision=lax.Precision.HIGHEST
    )
    totals = lax.psum(fwd_count + bwd_count, ("expert", "dp"))
    expert_load = lax.dynamic_slice_in_dim(totals, lax.axis_index("expert") // sharing, 1)[0]
    return (
        fwd_next.astype(jnp.bfloat16)[None],
        bwd_next.astype(jnp.bfloat16)[None],
        expert_load.reshape(1, 1),
    )


def solution(mesh):
    in_specs = (
        P("section", ("expert", "dp"), None),
        P("section", ("expert", "dp"), None),
        P("section", ("expert", "dp"), None),
        P("section", ("expert", "dp"), None),
        P("section", ("expert", "dp"), None),
        P("section", ("expert", "dp"), None),
        P("section", "dp", None, None, "expert"),
        P("section", None, "expert"),
        P("section", None, "expert"),
        P("section", "expert", None),
    )
    out_specs = (
        P("section", ("expert", "dp"), None),
        P("section", ("expert", "dp"), None),
        P("section", "expert"),
    )
    return jax.shard_map(shards, mesh=mesh, in_specs=in_specs, out_specs=out_specs, check_vma=False)
```

```python
import functools

import jax
import jax.numpy as jnp
from jax import lax
from jax.experimental import pallas as pl
from jax.experimental.pallas import tpu as pltpu
from jax.sharding import PartitionSpec as P

MESH = pl.DeviceIdType.MESH
LEFT, RIGHT = 0, 1
FWD, BWD = 0, 1
GATHER_CHUNKS = 4
RETURN_CHUNKS = 4


def from_behind(array, axis, by):
    length = lax.axis_size(axis)
    return lax.ppermute(array, axis, [(i, (i + by) % length) for i in range(length)])


def slot_tables(routes, probs, exp_count, capacity):
    slot_count = exp_count * capacity
    flat_routes = routes.reshape(-1)
    onehot = (flat_routes[:, None] == jnp.arange(exp_count, dtype=jnp.int32)[None, :]).astype(
        jnp.int32
    )
    before = jnp.cumsum(onehot, axis=0) - onehot
    position = jnp.sum(before * onehot, axis=1)
    slot_ids = flat_routes * capacity + position
    matches = (slot_ids[:, None] == jnp.arange(slot_count, dtype=jnp.int32)[None, :]).astype(
        jnp.float32
    )
    matches = matches.reshape(routes.shape[0], routes.shape[1], slot_count)
    placing = jnp.sum(matches, axis=1)
    weighing = jnp.sum(matches * probs[:, :, None], axis=1)
    counted = jnp.sum(onehot, axis=0)
    return (placing, weighing, counted)


def cuts(width, wanted, small_first):
    unit = 256
    count = width // unit
    pieces = min(wanted, count)
    sizes = [count // pieces + (1 if i < count % pieces else 0) for i in range(pieces)]
    if small_first:
        sizes = sizes[::-1]
    starts = [sum(sizes[:i]) for i in range(pieces)]
    return [pl.ds(a * unit, b * unit) for a, b in zip(starts, sizes)]


def relay_kernel(
    size,
    x_hbm,
    cot_hbm,
    f_routes,
    b_routes,
    f_probs,
    b_probs,
    saved_hbm,
    gate_hbm,
    up_hbm,
    down_hbm,
    f_out,
    b_out,
    load_out,
    gate_w,
    up_w,
    down_w,
    saved,
    x_own,
    rows_all,
    meta,
    from_right,
    from_left,
    going,
    part,
    hidden_acc,
    mid,
    w_sem,
    shift_send,
    shift_recv,
    meta_send,
    meta_recv,
    g_send,
    g_recv,
    r_send,
    r_recv,
):
    n, n_dp, n_sec, sharing, cap, rows = size
    group = n * n_dp
    width = cot_hbm.shape[1]
    me = lax.axis_index("expert")
    dp = lax.axis_index("dp")
    sec = lax.axis_index("section")
    lin = me * n_dp + dp
    g_cuts = cuts(width, GATHER_CHUNKS, False)
    r_cuts = cuts(width, RETURN_CHUNKS, True)
    contract_last = (((1,), (1,)), ((), ()))

    def place(block):
        return pl.ds(pl.multiple_of(block * rows, rows), rows)

    own_rows = [
        pltpu.make_async_copy(x_hbm, x_own, w_sem.at[4]),
        pltpu.make_async_copy(cot_hbm, rows_all.at[BWD, place(me), :], w_sem.at[5]),
    ]
    for load in own_rows:
        load.start()
    loads = [
        pltpu.make_async_copy(down_hbm, down_w, w_sem.at[0]),
        pltpu.make_async_copy(saved_hbm, saved, w_sem.at[1]),
        pltpu.make_async_copy(gate_hbm, gate_w, w_sem.at[2]),
        pltpu.make_async_copy(up_hbm, up_w, w_sem.at[3]),
    ]
    for load in loads[:2]:
        load.start()

    barrier = pltpu.get_barrier_semaphore()

    def peer(off):
        other = lax.rem(lin + off, group)
        return {"expert": lax.div(other, n_dp), "dp": lax.rem(other, n_dp)}

    for off in range(1, group):
        pl.semaphore_signal(barrier, inc=1, device_id=peer(off), device_id_type=MESH)
    pl.semaphore_signal(
        barrier,
        inc=1,
        device_id={"section": lax.rem(sec + n_sec - 1, n_sec)},
        device_id_type=MESH,
    )

    at_row = lax.broadcasted_iota(jnp.int32, (rows, rows), 0)
    at_col = lax.broadcasted_iota(jnp.int32, (rows, rows), 1)
    eye = at_row == at_col

    def column(line):
        spread = jnp.where(eye, jnp.broadcast_to(line, (rows, rows)), 0.0)
        return jnp.sum(spread, axis=1, keepdims=True)

    meta[lin] = jnp.zeros(meta.shape[1:], jnp.float32)
    for span, routes in ((FWD, f_routes), (BWD, b_routes)):
        named_row = routes[...].astype(jnp.float32)
        named = column(named_row)
        earlier = jnp.where((named == named_row) & (at_row < at_col), 1.0, 0.0)
        slot = named_row * cap + jnp.sum(earlier, axis=0, keepdims=True)
        meta[lin, span : span + 1, 0:rows] = slot
    pl.semaphore_wait(barrier, group)

    def gather_copy(span, way, hop, chunk):
        block = me - (hop - 1) if way == RIGHT else me + (hop - 1)
        there = me + 1 if way == RIGHT else me - 1
        piece = rows_all.at[span, place(block), g_cuts[chunk]]
        return pltpu.make_async_remote_copy(
            src_ref=piece,
            dst_ref=piece,
            send_sem=g_send.at[span, way, hop - 1, chunk],
            recv_sem=g_recv.at[span, way, hop - 1, chunk],
            device_id={"expert": there},
            device_id_type=MESH,
        )

    def gather_sends(way, hop):
        if way == RIGHT:
            return (me >= hop - 1) & (me < n - 1)
        return (me <= n - hop) & (me > 0)

    def gather_wait(span, way, hop, chunk):
        block = me - hop if way == RIGHT else me + hop
        there = me - 1 if way == RIGHT else me + 1
        piece = rows_all.at[span, place(block), g_cuts[chunk]]
        pltpu.make_async_remote_copy(
            src_ref=piece,
            dst_ref=piece,
            send_sem=g_send.at[span, way, hop - 1, chunk],
            recv_sem=g_recv.at[span, way, hop - 1, chunk],
            device_id={"expert": there},
            device_id_type=MESH,
        ).wait_recv()

    def gather_start(span, hop, chunk):
        for way in (LEFT, RIGHT):

            @pl.when(gather_sends(way, hop))
            def _():
                gather_copy(span, way, hop, chunk).start()

    def gather_step(span, hop, chunk):
        for way in (LEFT, RIGHT):
            there = me >= hop if way == RIGHT else me + hop < n

            @pl.when(there)
            def _():
                gather_wait(span, way, hop, chunk)

            if hop < n - 1:

                @pl.when(gather_sends(way, hop + 1))
                def _():
                    gather_copy(span, way, hop + 1, chunk).start()

    def return_copy(span, way, block, chunk):
        landing = from_left if way == RIGHT else from_right
        there = me + 1 if way == RIGHT else me - 1
        spot = pl.ds(block * rows, rows)
        return pltpu.make_async_remote_copy(
            src_ref=going.at[span, spot, r_cuts[chunk]],
            dst_ref=landing.at[span, spot, r_cuts[chunk]],
            send_sem=r_send.at[span, way, block, chunk],
            recv_sem=r_recv.at[span, way, block, chunk],
            device_id={"expert": there},
            device_id_type=MESH,
        )

    def return_wait(span, way, block, chunk):
        landing = from_left if way == RIGHT else from_right
        there = me - 1 if way == RIGHT else me + 1
        piece = landing.at[span, place(block), r_cuts[chunk]]
        pltpu.make_async_remote_copy(
            src_ref=piece,
            dst_ref=piece,
            send_sem=r_send.at[span, way, block, chunk],
            recv_sem=r_recv.at[span, way, block, chunk],
            device_id={"expert": there},
            device_id_type=MESH,
        ).wait_recv()

    def return_step(span, hop, chunk):
        for way in (LEFT, RIGHT):
            at = n - 1 - hop if way == LEFT else hop
            blocks = range(at) if way == LEFT else range(n - 1, at, -1)
            landing = from_left if way == RIGHT else from_right

            @pl.when(me == at)
            def _():
                for block in blocks:
                    spot = pl.ds(block * rows, rows)
                    total = part[span, spot, r_cuts[chunk]]
                    if hop > 0:
                        return_wait(span, way, block, chunk)
                        total = total + landing[span, spot, r_cuts[chunk]].astype(jnp.float32)
                    going[span, spot, r_cuts[chunk]] = total.astype(jnp.bfloat16)
                    return_copy(span, way, block, chunk).start()

    def finish(span, chunk, base, probs, out):
        spot = place(me)
        for way in (LEFT, RIGHT):
            landing = from_left if way == RIGHT else from_right
            there = me > 0 if way == RIGHT else me < n - 1

            @pl.when(there)
            def _():
                return_wait(span, way, me, chunk)
                part[span, spot, r_cuts[chunk]] += landing[span, spot, r_cuts[chunk]].astype(
                    jnp.float32
                )

        out[:, r_cuts[chunk]] = (
            base(r_cuts[chunk]).astype(jnp.float32)
            + column(probs[...]) * part[span, spot, r_cuts[chunk]]
        )

    def meta_copy(off):
        return pltpu.make_async_remote_copy(
            src_ref=meta.at[lin],
            dst_ref=meta.at[lin],
            send_sem=meta_send.at[off],
            recv_sem=meta_recv.at[off],
            device_id=peer(off),
            device_id_type=MESH,
        )

    def meta_wait(off):
        other = meta.at[lax.rem(lin + group - off, group)]
        pltpu.make_async_remote_copy(
            src_ref=other,
            dst_ref=other,
            send_sem=meta_send.at[off],
            recv_sem=meta_recv.at[off],
            device_id=peer(group - off),
            device_id_type=MESH,
        ).wait_recv()

    def shift_copy(chunk):
        return pltpu.make_async_remote_copy(
            src_ref=x_own.at[:, g_cuts[chunk]],
            dst_ref=rows_all.at[FWD, place(me), g_cuts[chunk]],
            send_sem=shift_send.at[chunk],
            recv_sem=shift_recv.at[chunk],
            device_id={"section": lax.rem(sec + 1, n_sec)},
            device_id_type=MESH,
        )

    own_rows[0].wait()
    for chunk in range(len(g_cuts)):
        shift_copy(chunk).start()
    own_rows[1].wait()
    for chunk in range(len(g_cuts)):
        gather_start(BWD, 1, chunk)
    for load in loads[2:]:
        load.start()
    for off in range(1, group):
        meta_copy(off).start()

    for hop in range(1, n - 1):
        for chunk in range(len(g_cuts)):
            gather_step(BWD, hop, chunk)
        if hop == 1:
            for off in range(1, group):
                meta_wait(off)
            first = (lax.div(me, sharing) * cap).astype(jnp.float32)
            owned = jnp.zeros((2, rows), jnp.float32)
            for other in range(group):
                slots = meta[other, 0:2, 0:rows] - first
                owned = owned + jnp.where((slots >= 0.0) & (slots < cap), 1.0, 0.0)
            owned = jnp.sum(jnp.sum(owned, axis=1, keepdims=True), axis=0, keepdims=True)
            load_out[...] = owned.astype(jnp.int32)

            def slots_of(span, block):
                line = meta[block * n_dp + dp, span : span + 1, 0:rows] - first
                return column(line)

            lanes = lax.broadcasted_iota(jnp.int32, (rows, n * cap), 1).astype(jnp.float32)
            taken = []
            for block in range(n):
                slots = slots_of(BWD, block)
                hit = (slots >= 0.0) & (slots < cap) & (lanes == slots + block * cap)
                taken.append(jnp.where(hit, 1.0, 0.0))
            taken = jnp.concatenate(taken, axis=0).astype(jnp.bfloat16)
            kept = []
            for block in range(n):
                slots = slots_of(FWD, block)
                kept.append(jnp.where((slots >= 0.0) & (slots < cap), 1.0, 0.0))
            kept = jnp.concatenate(kept, axis=0) > 0.5
            loads[1].wait()
            stored = saved[...].astype(jnp.float32)
            saved_gate = jnp.dot(
                taken, stored[:, 0, :].astype(jnp.bfloat16), preferred_element_type=jnp.float32
            )
            saved_up = jnp.dot(
                taken, stored[:, 1, :].astype(jnp.bfloat16), preferred_element_type=jnp.float32
            )
            sigma = jax.nn.sigmoid(saved_gate)
            hidden_acc[0] = saved_up * sigma * (1.0 + saved_gate * (1.0 - sigma))
            hidden_acc[1] = saved_gate * sigma

    loads[0].wait()
    for chunk, cut in enumerate(g_cuts):
        gather_step(BWD, n - 1, chunk)
        term = lax.dot_general(
            rows_all[BWD, :, cut],
            down_w[:, cut],
            contract_last,
            preferred_element_type=jnp.float32,
        )
        if chunk == 0:
            hidden_acc[2] = term
        else:
            hidden_acc[2] += term
    mid[0] = (hidden_acc[2] * hidden_acc[0]).astype(jnp.bfloat16)
    mid[1] = (hidden_acc[2] * hidden_acc[1]).astype(jnp.bfloat16)

    for chunk in range(len(g_cuts)):
        shift_copy(chunk).wait_recv()
        gather_start(FWD, 1, chunk)
    loads[2].wait()
    loads[3].wait()

    def bwd_part(chunk):
        cut = r_cuts[chunk]
        part[BWD, :, cut] = lax.dot_general(
            mid[0], gate_w[cut, :], contract_last, preferred_element_type=jnp.float32
        ) + lax.dot_general(
            mid[1], up_w[cut, :], contract_last, preferred_element_type=jnp.float32
        )

    r_count, g_count = len(r_cuts), len(g_cuts)
    for chunk in range(max(r_count, g_count)):
        if chunk < r_count:
            bwd_part(chunk)
            return_step(BWD, 0, chunk)
        if chunk < g_count:
            gather_step(FWD, 1, chunk)
    for hop in range(1, n - 1):
        for chunk in range(max(r_count, g_count)):
            if chunk < g_count and hop + 1 < n - 1:
                gather_step(FWD, hop + 1, chunk)
            if chunk < r_count:
                return_step(BWD, hop, chunk)

    for chunk, cut in enumerate(g_cuts):
        if n > 2:
            gather_step(FWD, n - 1, chunk)
        for at, weights in ((0, gate_w), (1, up_w)):
            term = jnp.dot(
                rows_all[FWD, :, cut], weights[cut, :], preferred_element_type=jnp.float32
            )
            if chunk == 0:
                hidden_acc[at] = term
            else:
                hidden_acc[at] += term
    activated = jax.nn.silu(hidden_acc[0]) * hidden_acc[1]
    mid[0] = jnp.where(kept, activated, 0.0).astype(jnp.bfloat16)

    for chunk in range(r_count):
        cut = r_cuts[chunk]
        part[FWD, :, cut] = jnp.dot(mid[0], down_w[:, cut], preferred_element_type=jnp.float32)
        return_step(FWD, 0, chunk)
    for chunk in range(r_count):
        finish(BWD, chunk, lambda cut: rows_all[BWD, place(me), cut], b_probs, b_out)
    for hop in range(1, n - 1):
        for chunk in range(r_count):
            return_step(FWD, hop, chunk)
    for chunk in range(r_count):
        finish(FWD, chunk, lambda cut: rows_all[FWD, place(me), cut], f_probs, f_out)

    for chunk in range(len(g_cuts)):
        shift_copy(chunk).wait_send()
    for off in range(1, group):
        meta_copy(off).wait_send()
    for span in (BWD, FWD):
        for way in (LEFT, RIGHT):
            for hop in range(1, n):

                @pl.when(gather_sends(way, hop))
                def _():
                    for chunk in range(len(g_cuts)):
                        gather_copy(span, way, hop, chunk).wait_send()

            for block in range(n):

                @pl.when(me > block if way == LEFT else me < block)
                def _():
                    for chunk in range(r_count):
                        return_copy(span, way, block, chunk).wait_send()


def relay_fits(fwd_sent, top_count, capacity):
    rows, width = fwd_sent.shape[1:]
    return (
        top_count == 1
        and capacity == rows
        and rows % 16 == 0
        and rows <= 128
        and width % 256 == 0
        and lax.axis_size("expert") > 2
        and lax.axis_size("section") > 1
    )


def relay(
    fwd_sent,
    fwd_routes,
    fwd_probs,
    backward_cotangent,
    bwd_routes,
    bwd_probs,
    saved_pre,
    w_gate,
    w_up,
    w_down,
    *,
    sharing,
    capacity,
):
    n, n_dp, n_sec = (lax.axis_size(name) for name in ("expert", "dp", "section"))
    rows, width = fwd_sent.shape[1:]
    hidden = w_gate.shape[2]
    tokens = n * rows
    bf16, f32 = jnp.bfloat16, jnp.float32
    group = n * n_dp
    g_count = len(cuts(width, GATHER_CHUNKS, False))
    r_count = len(cuts(width, RETURN_CHUNKS, True))
    vmem = pl.BlockSpec(memory_space=pltpu.VMEM)
    hbm = pl.BlockSpec(memory_space=pl.ANY)
    f_next, b_next, load = pl.pallas_call(
        functools.partial(relay_kernel, (n, n_dp, n_sec, sharing, capacity, rows)),
        out_shape=(
            jax.ShapeDtypeStruct((rows, width), f32),
            jax.ShapeDtypeStruct((rows, width), f32),
            jax.ShapeDtypeStruct((1, 1), jnp.int32),
        ),
        in_specs=[hbm] * 2 + [vmem] * 4 + [hbm] * 4,
        out_specs=(vmem, vmem, vmem),
        scratch_shapes=[
            pltpu.VMEM((width, hidden), bf16),
            pltpu.VMEM((width, hidden), bf16),
            pltpu.VMEM((hidden, width), bf16),
            pltpu.VMEM(saved_pre.shape[2:], bf16),
            pltpu.VMEM((rows, width), bf16),
            pltpu.VMEM((2, tokens, width), bf16),
            pltpu.VMEM((group, 8, 128), f32),
            pltpu.VMEM((2, tokens, width), bf16),
            pltpu.VMEM((2, tokens, width), bf16),
            pltpu.VMEM((2, tokens, width), bf16),
            pltpu.VMEM((2, tokens, width), f32),
            pltpu.VMEM((3, tokens, hidden), f32),
            pltpu.VMEM((2, tokens, hidden), bf16),
            pltpu.SemaphoreType.DMA((6,)),
            pltpu.SemaphoreType.DMA((g_count,)),
            pltpu.SemaphoreType.DMA((g_count,)),
            pltpu.SemaphoreType.DMA((group,)),
            pltpu.SemaphoreType.DMA((group,)),
            pltpu.SemaphoreType.DMA((2, 2, n - 1, g_count)),
            pltpu.SemaphoreType.DMA((2, 2, n - 1, g_count)),
            pltpu.SemaphoreType.DMA((2, 2, n, r_count)),
            pltpu.SemaphoreType.DMA((2, 2, n, r_count)),
        ],
        compiler_params=pltpu.CompilerParams(
            collective_id=0, has_side_effects=True, vmem_limit_bytes=60 * 1024 * 1024
        ),
        cost_estimate=pl.CostEstimate(
            flops=12 * tokens * width * hidden,
            bytes_accessed=6 * width * hidden,
            transcendentals=2 * tokens * hidden,
        ),
    )(
        fwd_sent[0],
        backward_cotangent[0],
        fwd_routes.reshape(1, rows),
        bwd_routes.reshape(1, rows),
        fwd_probs.reshape(1, rows),
        bwd_probs.reshape(1, rows),
        saved_pre[0, 0],
        w_gate[0],
        w_up[0],
        w_down[0],
    )
    return f_next.astype(bf16)[None], b_next.astype(bf16)[None], load


def shards(
    fwd_sent,
    fwd_routes,
    fwd_probs,
    backward_cotangent,
    bwd_routes,
    bwd_probs,
    saved_pre,
    w_gate,
    w_up,
    w_down,
):
    experts = lax.axis_size("expert")
    sharing = min(4, experts // 2)
    exp_count = experts // sharing
    token_rows = fwd_sent.shape[1]
    top_count = fwd_routes.shape[2]
    capacity = min(token_rows, max(2, 2 * token_rows * top_count // exp_count))
    slot_count = experts * capacity
    if relay_fits(fwd_sent, top_count, capacity):
        return relay(
            fwd_sent,
            fwd_routes,
            fwd_probs,
            backward_cotangent,
            bwd_routes,
            bwd_probs,
            saved_pre,
            w_gate,
            w_up,
            w_down,
            sharing=sharing,
            capacity=capacity,
        )
    arrived = from_behind(fwd_sent, "section", 1)[0]
    gate_mat = w_gate[0]
    up_mat = w_up[0]
    down_mat = w_down[0]
    stored = saved_pre[0, 0]
    cotangent = backward_cotangent[0]
    fwd_place, fwd_weigh, fwd_count = slot_tables(fwd_routes[0], fwd_probs[0], exp_count, capacity)
    bwd_place, bwd_weigh, bwd_count = slot_tables(bwd_routes[0], bwd_probs[0], exp_count, capacity)

    def forward_rows(slot_rows):
        gate_pre = jnp.dot(slot_rows, gate_mat, preferred_element_type=jnp.float32)
        up_pre = jnp.dot(slot_rows, up_mat, preferred_element_type=jnp.float32)
        hidden_state = (jax.nn.silu(gate_pre) * up_pre).astype(jnp.bfloat16)
        return jnp.dot(hidden_state, down_mat, preferred_element_type=jnp.float32).astype(
            jnp.bfloat16
        )

    def backward_rows(slot_rows):
        contract = (((1,), (1,)), ((), ()))
        grad_hidden = lax.dot_general(
            slot_rows, down_mat, contract, preferred_element_type=jnp.float32
        )
        saved_gate = stored[:, 0].astype(jnp.float32)
        saved_up = stored[:, 1].astype(jnp.float32)
        sigma = jax.nn.sigmoid(saved_gate)
        grad_gate = (grad_hidden * saved_up * sigma * (1.0 + saved_gate * (1.0 - sigma))).astype(
            jnp.bfloat16
        )
        grad_up = (grad_hidden * saved_gate * sigma).astype(jnp.bfloat16)
        summed = lax.dot_general(grad_gate, gate_mat, contract, preferred_element_type=jnp.float32)
        summed = summed + lax.dot_general(
            grad_up, up_mat, contract, preferred_element_type=jnp.float32
        )
        return summed.astype(jnp.bfloat16)

    def send_rows(tokens, placing):
        width = tokens.shape[1]
        outgoing = jnp.dot(
            placing.T.astype(jnp.bfloat16), tokens, preferred_element_type=jnp.float32
        )
        outgoing = outgoing.astype(jnp.bfloat16).reshape(exp_count, 1, capacity, width)
        outgoing = jnp.broadcast_to(outgoing, (exp_count, sharing, capacity, width)).reshape(
            experts, capacity, width
        )
        received = lax.all_to_all(outgoing, "expert", split_axis=0, concat_axis=0, tiled=True)
        owned = jnp.zeros((), jnp.int32)
        return (received.reshape(slot_count, width), owned)

    def finish_rows(received, compute):
        width = received.shape[1]
        result_list = compute(received)
        returned = lax.all_to_all(
            result_list.reshape(experts, capacity, width),
            "expert",
            split_axis=0,
            concat_axis=0,
            tiled=True,
        )
        gathered = jnp.sum(
            returned.reshape(exp_count, sharing, capacity, width).astype(jnp.float32), axis=1
        )
        return gathered.reshape(exp_count * capacity, width)

    fwd_rows, fwd_owned = send_rows(arrived, fwd_place)
    fwd_back = finish_rows(fwd_rows, forward_rows)
    bwd_rows, bwd_owned = send_rows(cotangent, bwd_place)
    bwd_back = finish_rows(bwd_rows, backward_rows)
    fwd_next = arrived.astype(jnp.float32) + jnp.dot(
        fwd_weigh, fwd_back, precision=lax.Precision.HIGHEST
    )
    bwd_next = cotangent.astype(jnp.float32) + jnp.dot(
        bwd_weigh, bwd_back, precision=lax.Precision.HIGHEST
    )
    totals = lax.psum(fwd_count + bwd_count, ("expert", "dp"))
    expert_load = lax.dynamic_slice_in_dim(totals, lax.axis_index("expert") // sharing, 1)[0]
    return (
        fwd_next.astype(jnp.bfloat16)[None],
        bwd_next.astype(jnp.bfloat16)[None],
        expert_load.reshape(1, 1),
    )


def solution(mesh):
    in_specs = (
        P("section", ("expert", "dp"), None),
        P("section", ("expert", "dp"), None),
        P("section", ("expert", "dp"), None),
        P("section", ("expert", "dp"), None),
        P("section", ("expert", "dp"), None),
        P("section", ("expert", "dp"), None),
        P("section", "dp", None, None, "expert"),
        P("section", None, "expert"),
        P("section", None, "expert"),
        P("section", "expert", None),
    )
    out_specs = (
        P("section", ("expert", "dp"), None),
        P("section", ("expert", "dp"), None),
        P("section", "expert"),
    )
    return jax.shard_map(shards, mesh=mesh, in_specs=in_specs, out_specs=out_specs, check_vma=False)
```

```python
import functools

import jax
import jax.numpy as jnp
from jax import lax
from jax.experimental import pallas as pl
from jax.experimental.pallas import tpu as pltpu
from jax.sharding import PartitionSpec as P

MESH = pl.DeviceIdType.MESH
LEFT, RIGHT = 0, 1
FWD, BWD = 0, 1
GATHER_CHUNKS = 4
RETURN_CHUNKS = 4


def from_behind(array, axis, by):
    length = lax.axis_size(axis)
    return lax.ppermute(array, axis, [(i, (i + by) % length) for i in range(length)])


def slot_tables(routes, probs, exp_count, capacity):
    slot_count = exp_count * capacity
    flat_routes = routes.reshape(-1)
    onehot = (flat_routes[:, None] == jnp.arange(exp_count, dtype=jnp.int32)[None, :]).astype(
        jnp.int32
    )
    before = jnp.cumsum(onehot, axis=0) - onehot
    position = jnp.sum(before * onehot, axis=1)
    slot_ids = flat_routes * capacity + position
    matches = (slot_ids[:, None] == jnp.arange(slot_count, dtype=jnp.int32)[None, :]).astype(
        jnp.float32
    )
    matches = matches.reshape(routes.shape[0], routes.shape[1], slot_count)
    placing = jnp.sum(matches, axis=1)
    weighing = jnp.sum(matches * probs[:, :, None], axis=1)
    counted = jnp.sum(onehot, axis=0)
    return (placing, weighing, counted)


def cuts(width, wanted, small_first):
    unit = 256
    count = width // unit
    pieces = min(wanted, count)
    sizes = [count // pieces + (1 if i < count % pieces else 0) for i in range(pieces)]
    if small_first:
        sizes = sizes[::-1]
    starts = [sum(sizes[:i]) for i in range(pieces)]
    return [pl.ds(a * unit, b * unit) for a, b in zip(starts, sizes)]


def relay_kernel(
    size,
    x_hbm,
    cot_hbm,
    f_routes,
    b_routes,
    f_probs,
    b_probs,
    saved_hbm,
    gate_hbm,
    up_hbm,
    down_hbm,
    f_out,
    b_out,
    load_out,
    gate_w,
    up_w,
    down_w,
    saved,
    x_own,
    rows_all,
    meta,
    from_right,
    from_left,
    going,
    part,
    hidden_acc,
    grad_acc,
    mid,
    w_sem,
    shift_send,
    shift_recv,
    meta_send,
    meta_recv,
    g_send,
    g_recv,
    r_send,
    r_recv,
):
    n, n_dp, n_sec, sharing, cap, rows = size
    group = n * n_dp
    width = cot_hbm.shape[1]
    me = lax.axis_index("expert")
    dp = lax.axis_index("dp")
    sec = lax.axis_index("section")
    lin = me * n_dp + dp
    g_cuts = cuts(width, GATHER_CHUNKS, False)
    r_cuts = cuts(width, RETURN_CHUNKS, True)
    contract_last = (((1,), (1,)), ((), ()))

    def place(block):
        return pl.ds(pl.multiple_of(block * rows, rows), rows)

    own_rows = [
        pltpu.make_async_copy(x_hbm, x_own, w_sem.at[4]),
        pltpu.make_async_copy(cot_hbm, rows_all.at[BWD, place(me), :], w_sem.at[5]),
    ]
    for load in own_rows:
        load.start()
    loads = [
        pltpu.make_async_copy(down_hbm, down_w, w_sem.at[0]),
        pltpu.make_async_copy(saved_hbm, saved, w_sem.at[1]),
        pltpu.make_async_copy(gate_hbm, gate_w, w_sem.at[2]),
        pltpu.make_async_copy(up_hbm, up_w, w_sem.at[3]),
    ]
    for load in loads[:2]:
        load.start()

    barrier = pltpu.get_barrier_semaphore()

    def peer(off):
        other = lax.rem(lin + off, group)
        return {"expert": lax.div(other, n_dp), "dp": lax.rem(other, n_dp)}

    for off in range(1, group):
        pl.semaphore_signal(barrier, inc=1, device_id=peer(off), device_id_type=MESH)
    pl.semaphore_signal(
        barrier,
        inc=1,
        device_id={"section": lax.rem(sec + n_sec - 1, n_sec)},
        device_id_type=MESH,
    )

    at_row = lax.broadcasted_iota(jnp.int32, (rows, rows), 0)
    at_col = lax.broadcasted_iota(jnp.int32, (rows, rows), 1)
    eye = at_row == at_col

    def column(line):
        spread = jnp.where(eye, jnp.broadcast_to(line, (rows, rows)), 0.0)
        return jnp.sum(spread, axis=1, keepdims=True)

    meta[lin] = jnp.zeros(meta.shape[1:], jnp.float32)
    for span, routes in ((FWD, f_routes), (BWD, b_routes)):
        named_row = routes[...].astype(jnp.float32)
        named = column(named_row)
        earlier = jnp.where((named == named_row) & (at_row < at_col), 1.0, 0.0)
        slot = named_row * cap + jnp.sum(earlier, axis=0, keepdims=True)
        meta[lin, span : span + 1, 0:rows] = slot
    pl.semaphore_wait(barrier, group)

    def gather_copy(span, way, hop, chunk):
        block = me - (hop - 1) if way == RIGHT else me + (hop - 1)
        there = me + 1 if way == RIGHT else me - 1
        piece = rows_all.at[span, place(block), g_cuts[chunk]]
        return pltpu.make_async_remote_copy(
            src_ref=piece,
            dst_ref=piece,
            send_sem=g_send.at[span, way, hop - 1, chunk],
            recv_sem=g_recv.at[span, way, hop - 1, chunk],
            device_id={"expert": there},
            device_id_type=MESH,
        )

    def gather_sends(way, hop):
        if way == RIGHT:
            return (me >= hop - 1) & (me < n - 1)
        return (me <= n - hop) & (me > 0)

    def gather_wait(span, way, hop, chunk):
        block = me - hop if way == RIGHT else me + hop
        there = me - 1 if way == RIGHT else me + 1
        piece = rows_all.at[span, place(block), g_cuts[chunk]]
        pltpu.make_async_remote_copy(
            src_ref=piece,
            dst_ref=piece,
            send_sem=g_send.at[span, way, hop - 1, chunk],
            recv_sem=g_recv.at[span, way, hop - 1, chunk],
            device_id={"expert": there},
            device_id_type=MESH,
        ).wait_recv()

    def gather_start(span, hop, chunk):
        for way in (LEFT, RIGHT):

            @pl.when(gather_sends(way, hop))
            def _():
                gather_copy(span, way, hop, chunk).start()

    def gather_step(span, hop, chunk):
        for way in (LEFT, RIGHT):
            there = me >= hop if way == RIGHT else me + hop < n

            @pl.when(there)
            def _():
                gather_wait(span, way, hop, chunk)

            if hop < n - 1:

                @pl.when(gather_sends(way, hop + 1))
                def _():
                    gather_copy(span, way, hop + 1, chunk).start()

    def return_copy(span, way, block, chunk):
        landing = from_left if way == RIGHT else from_right
        there = me + 1 if way == RIGHT else me - 1
        spot = pl.ds(block * rows, rows)
        return pltpu.make_async_remote_copy(
            src_ref=going.at[span, spot, r_cuts[chunk]],
            dst_ref=landing.at[span, spot, r_cuts[chunk]],
            send_sem=r_send.at[span, way, block, chunk],
            recv_sem=r_recv.at[span, way, block, chunk],
            device_id={"expert": there},
            device_id_type=MESH,
        )

    def return_wait(span, way, block, chunk):
        landing = from_left if way == RIGHT else from_right
        there = me - 1 if way == RIGHT else me + 1
        piece = landing.at[span, place(block), r_cuts[chunk]]
        pltpu.make_async_remote_copy(
            src_ref=piece,
            dst_ref=piece,
            send_sem=r_send.at[span, way, block, chunk],
            recv_sem=r_recv.at[span, way, block, chunk],
            device_id={"expert": there},
            device_id_type=MESH,
        ).wait_recv()

    def return_step(span, hop, chunk):
        for way in (LEFT, RIGHT):
            at = n - 1 - hop if way == LEFT else hop
            blocks = range(at) if way == LEFT else range(n - 1, at, -1)
            landing = from_left if way == RIGHT else from_right

            @pl.when(me == at)
            def _():
                for block in blocks:
                    spot = pl.ds(block * rows, rows)
                    total = part[span, spot, r_cuts[chunk]]
                    if hop > 0:
                        return_wait(span, way, block, chunk)
                        total = total + landing[span, spot, r_cuts[chunk]].astype(jnp.float32)
                    going[span, spot, r_cuts[chunk]] = total.astype(jnp.bfloat16)
                    return_copy(span, way, block, chunk).start()

    def finish(span, chunk, base, probs, out):
        spot = place(me)
        for way in (LEFT, RIGHT):
            landing = from_left if way == RIGHT else from_right
            there = me > 0 if way == RIGHT else me < n - 1

            @pl.when(there)
            def _():
                return_wait(span, way, me, chunk)
                part[span, spot, r_cuts[chunk]] += landing[span, spot, r_cuts[chunk]].astype(
                    jnp.float32
                )

        out[:, r_cuts[chunk]] = (
            base(r_cuts[chunk]).astype(jnp.float32)
            + column(probs[...]) * part[span, spot, r_cuts[chunk]]
        )

    def meta_copy(off):
        return pltpu.make_async_remote_copy(
            src_ref=meta.at[lin],
            dst_ref=meta.at[lin],
            send_sem=meta_send.at[off],
            recv_sem=meta_recv.at[off],
            device_id=peer(off),
            device_id_type=MESH,
        )

    def meta_wait(off):
        other = meta.at[lax.rem(lin + group - off, group)]
        pltpu.make_async_remote_copy(
            src_ref=other,
            dst_ref=other,
            send_sem=meta_send.at[off],
            recv_sem=meta_recv.at[off],
            device_id=peer(group - off),
            device_id_type=MESH,
        ).wait_recv()

    def shift_copy(chunk):
        return pltpu.make_async_remote_copy(
            src_ref=x_own.at[:, g_cuts[chunk]],
            dst_ref=rows_all.at[FWD, place(me), g_cuts[chunk]],
            send_sem=shift_send.at[chunk],
            recv_sem=shift_recv.at[chunk],
            device_id={"section": lax.rem(sec + 1, n_sec)},
            device_id_type=MESH,
        )

    own_rows[0].wait()
    for chunk in range(len(g_cuts)):
        shift_copy(chunk).start()
    own_rows[1].wait()
    for chunk in range(len(g_cuts)):
        gather_start(BWD, 1, chunk)
    for load in loads[2:]:
        load.start()
    for off in range(1, group):
        meta_copy(off).start()

    for hop in range(1, n - 1):
        for chunk in range(len(g_cuts)):
            gather_step(BWD, hop, chunk)
        if hop == n - 2:
            for chunk in range(len(g_cuts)):
                shift_copy(chunk).wait_recv()
                gather_start(FWD, 1, chunk)
            for off in range(1, group):
                meta_wait(off)
            first = (lax.div(me, sharing) * cap).astype(jnp.float32)
            owned = jnp.zeros((2, rows), jnp.float32)
            for other in range(group):
                slots = meta[other, 0:2, 0:rows] - first
                owned = owned + jnp.where((slots >= 0.0) & (slots < cap), 1.0, 0.0)
            owned = jnp.sum(jnp.sum(owned, axis=1, keepdims=True), axis=0, keepdims=True)
            load_out[...] = owned.astype(jnp.int32)

            def slots_of(span, block):
                line = meta[block * n_dp + dp, span : span + 1, 0:rows] - first
                return column(line)

            lanes = lax.broadcasted_iota(jnp.int32, (rows, n * cap), 1).astype(jnp.float32)
            taken = []
            for block in range(n):
                slots = slots_of(BWD, block)
                hit = (slots >= 0.0) & (slots < cap) & (lanes == slots + block * cap)
                taken.append(jnp.where(hit, 1.0, 0.0))
            taken = jnp.concatenate(taken, axis=0).astype(jnp.bfloat16)
            kept = []
            for block in range(n):
                slots = slots_of(FWD, block)
                kept.append(jnp.where((slots >= 0.0) & (slots < cap), 1.0, 0.0))
            kept = jnp.concatenate(kept, axis=0) > 0.5
            loads[1].wait()
            stored = saved[...].astype(jnp.float32)
            saved_gate = jnp.dot(
                taken, stored[:, 0, :].astype(jnp.bfloat16), preferred_element_type=jnp.float32
            )
            saved_up = jnp.dot(
                taken, stored[:, 1, :].astype(jnp.bfloat16), preferred_element_type=jnp.float32
            )
            sigma = jax.nn.sigmoid(saved_gate)
            hidden_acc[0] = saved_up * sigma * (1.0 + saved_gate * (1.0 - sigma))
            hidden_acc[1] = saved_gate * sigma

    loads[0].wait()
    for chunk, cut in enumerate(g_cuts):
        gather_step(BWD, n - 1, chunk)
        term = lax.dot_general(
            down_w[:, cut],
            rows_all[BWD, :, cut],
            contract_last,
            preferred_element_type=jnp.float32,
        )
        if chunk == 0:
            grad_acc[...] = term
        else:
            grad_acc[...] += term
    grad_hidden = grad_acc[...].T
    mid[0] = (grad_hidden * hidden_acc[0]).astype(jnp.bfloat16)
    mid[1] = (grad_hidden * hidden_acc[1]).astype(jnp.bfloat16)

    loads[2].wait()
    loads[3].wait()

    def bwd_part(chunk):
        cut = r_cuts[chunk]
        turned = lax.dot_general(
            gate_w[cut, :], mid[0], contract_last, preferred_element_type=jnp.float32
        ) + lax.dot_general(
            up_w[cut, :], mid[1], contract_last, preferred_element_type=jnp.float32
        )
        part[BWD, :, cut] = turned.T

    r_count, g_count = len(r_cuts), len(g_cuts)
    for chunk in range(max(r_count, g_count)):
        if chunk < r_count:
            bwd_part(chunk)
            return_step(BWD, 0, chunk)
        if chunk < g_count:
            gather_step(FWD, 1, chunk)
    for hop in range(1, n - 1):
        for chunk in range(max(r_count, g_count)):
            if chunk < g_count and hop + 1 < n - 1:
                gather_step(FWD, hop + 1, chunk)
            if chunk < r_count:
                return_step(BWD, hop, chunk)

    for chunk, cut in enumerate(g_cuts):
        if n > 2:
            gather_step(FWD, n - 1, chunk)
        for at, weights in ((0, gate_w), (1, up_w)):
            term = jnp.dot(
                rows_all[FWD, :, cut], weights[cut, :], preferred_element_type=jnp.float32
            )
            if chunk == 0:
                hidden_acc[at] = term
            else:
                hidden_acc[at] += term
    activated = jax.nn.silu(hidden_acc[0]) * hidden_acc[1]
    mid[0] = jnp.where(kept, activated, 0.0).astype(jnp.bfloat16)

    for chunk in range(r_count):
        cut = r_cuts[chunk]
        part[FWD, :, cut] = jnp.dot(mid[0], down_w[:, cut], preferred_element_type=jnp.float32)
        return_step(FWD, 0, chunk)
    for chunk in range(r_count):
        finish(BWD, chunk, lambda cut: rows_all[BWD, place(me), cut], b_probs, b_out)
    for hop in range(1, n - 1):
        for chunk in range(r_count):
            return_step(FWD, hop, chunk)
    for chunk in range(r_count):
        finish(FWD, chunk, lambda cut: rows_all[FWD, place(me), cut], f_probs, f_out)

    for chunk in range(len(g_cuts)):
        shift_copy(chunk).wait_send()
    for off in range(1, group):
        meta_copy(off).wait_send()
    for span in (BWD, FWD):
        for way in (LEFT, RIGHT):
            for hop in range(1, n):

                @pl.when(gather_sends(way, hop))
                def _():
                    for chunk in range(len(g_cuts)):
                        gather_copy(span, way, hop, chunk).wait_send()

            for block in range(n):

                @pl.when(me > block if way == LEFT else me < block)
                def _():
                    for chunk in range(r_count):
                        return_copy(span, way, block, chunk).wait_send()


def relay_fits(fwd_sent, top_count, capacity):
    rows, width = fwd_sent.shape[1:]
    return (
        top_count == 1
        and capacity == rows
        and rows % 16 == 0
        and rows <= 128
        and width % 256 == 0
        and lax.axis_size("expert") > 2
        and lax.axis_size("section") > 1
    )


def relay(
    fwd_sent,
    fwd_routes,
    fwd_probs,
    backward_cotangent,
    bwd_routes,
    bwd_probs,
    saved_pre,
    w_gate,
    w_up,
    w_down,
    *,
    sharing,
    capacity,
):
    n, n_dp, n_sec = (lax.axis_size(name) for name in ("expert", "dp", "section"))
    rows, width = fwd_sent.shape[1:]
    hidden = w_gate.shape[2]
    tokens = n * rows
    bf16, f32 = jnp.bfloat16, jnp.float32
    group = n * n_dp
    g_count = len(cuts(width, GATHER_CHUNKS, False))
    r_count = len(cuts(width, RETURN_CHUNKS, True))
    vmem = pl.BlockSpec(memory_space=pltpu.VMEM)
    hbm = pl.BlockSpec(memory_space=pl.ANY)
    f_next, b_next, load = pl.pallas_call(
        functools.partial(relay_kernel, (n, n_dp, n_sec, sharing, capacity, rows)),
        out_shape=(
            jax.ShapeDtypeStruct((rows, width), f32),
            jax.ShapeDtypeStruct((rows, width), f32),
            jax.ShapeDtypeStruct((1, 1), jnp.int32),
        ),
        in_specs=[hbm] * 2 + [vmem] * 4 + [hbm] * 4,
        out_specs=(vmem, vmem, vmem),
        scratch_shapes=[
            pltpu.VMEM((width, hidden), bf16),
            pltpu.VMEM((width, hidden), bf16),
            pltpu.VMEM((hidden, width), bf16),
            pltpu.VMEM(saved_pre.shape[2:], bf16),
            pltpu.VMEM((rows, width), bf16),
            pltpu.VMEM((2, tokens, width), bf16),
            pltpu.VMEM((group, 8, 128), f32),
            pltpu.VMEM((2, tokens, width), bf16),
            pltpu.VMEM((2, tokens, width), bf16),
            pltpu.VMEM((2, tokens, width), bf16),
            pltpu.VMEM((2, tokens, width), f32),
            pltpu.VMEM((2, tokens, hidden), f32),
            pltpu.VMEM((hidden, tokens), f32),
            pltpu.VMEM((2, tokens, hidden), bf16),
            pltpu.SemaphoreType.DMA((6,)),
            pltpu.SemaphoreType.DMA((g_count,)),
            pltpu.SemaphoreType.DMA((g_count,)),
            pltpu.SemaphoreType.DMA((group,)),
            pltpu.SemaphoreType.DMA((group,)),
            pltpu.SemaphoreType.DMA((2, 2, n - 1, g_count)),
            pltpu.SemaphoreType.DMA((2, 2, n - 1, g_count)),
            pltpu.SemaphoreType.DMA((2, 2, n, r_count)),
            pltpu.SemaphoreType.DMA((2, 2, n, r_count)),
        ],
        compiler_params=pltpu.CompilerParams(
            collective_id=0, has_side_effects=True, vmem_limit_bytes=60 * 1024 * 1024
        ),
        cost_estimate=pl.CostEstimate(
            flops=12 * tokens * width * hidden,
            bytes_accessed=6 * width * hidden,
            transcendentals=2 * tokens * hidden,
        ),
    )(
        fwd_sent[0],
        backward_cotangent[0],
        fwd_routes.reshape(1, rows),
        bwd_routes.reshape(1, rows),
        fwd_probs.reshape(1, rows),
        bwd_probs.reshape(1, rows),
        saved_pre[0, 0],
        w_gate[0],
        w_up[0],
        w_down[0],
    )
    return f_next.astype(bf16)[None], b_next.astype(bf16)[None], load


def shards(
    fwd_sent,
    fwd_routes,
    fwd_probs,
    backward_cotangent,
    bwd_routes,
    bwd_probs,
    saved_pre,
    w_gate,
    w_up,
    w_down,
):
    experts = lax.axis_size("expert")
    sharing = min(4, experts // 2)
    exp_count = experts // sharing
    token_rows = fwd_sent.shape[1]
    top_count = fwd_routes.shape[2]
    capacity = min(token_rows, max(2, 2 * token_rows * top_count // exp_count))
    slot_count = experts * capacity
    if relay_fits(fwd_sent, top_count, capacity):
        return relay(
            fwd_sent,
            fwd_routes,
            fwd_probs,
            backward_cotangent,
            bwd_routes,
            bwd_probs,
            saved_pre,
            w_gate,
            w_up,
            w_down,
            sharing=sharing,
            capacity=capacity,
        )
    arrived = from_behind(fwd_sent, "section", 1)[0]
    gate_mat = w_gate[0]
    up_mat = w_up[0]
    down_mat = w_down[0]
    stored = saved_pre[0, 0]
    cotangent = backward_cotangent[0]
    fwd_place, fwd_weigh, fwd_count = slot_tables(fwd_routes[0], fwd_probs[0], exp_count, capacity)
    bwd_place, bwd_weigh, bwd_count = slot_tables(bwd_routes[0], bwd_probs[0], exp_count, capacity)

    def forward_rows(slot_rows):
        gate_pre = jnp.dot(slot_rows, gate_mat, preferred_element_type=jnp.float32)
        up_pre = jnp.dot(slot_rows, up_mat, preferred_element_type=jnp.float32)
        hidden_state = (jax.nn.silu(gate_pre) * up_pre).astype(jnp.bfloat16)
        return jnp.dot(hidden_state, down_mat, preferred_element_type=jnp.float32).astype(
            jnp.bfloat16
        )

    def backward_rows(slot_rows):
        contract = (((1,), (1,)), ((), ()))
        grad_hidden = lax.dot_general(
            slot_rows, down_mat, contract, preferred_element_type=jnp.float32
        )
        saved_gate = stored[:, 0].astype(jnp.float32)
        saved_up = stored[:, 1].astype(jnp.float32)
        sigma = jax.nn.sigmoid(saved_gate)
        grad_gate = (grad_hidden * saved_up * sigma * (1.0 + saved_gate * (1.0 - sigma))).astype(
            jnp.bfloat16
        )
        grad_up = (grad_hidden * saved_gate * sigma).astype(jnp.bfloat16)
        summed = lax.dot_general(grad_gate, gate_mat, contract, preferred_element_type=jnp.float32)
        summed = summed + lax.dot_general(
            grad_up, up_mat, contract, preferred_element_type=jnp.float32
        )
        return summed.astype(jnp.bfloat16)

    def send_rows(tokens, placing):
        width = tokens.shape[1]
        outgoing = jnp.dot(
            placing.T.astype(jnp.bfloat16), tokens, preferred_element_type=jnp.float32
        )
        outgoing = outgoing.astype(jnp.bfloat16).reshape(exp_count, 1, capacity, width)
        outgoing = jnp.broadcast_to(outgoing, (exp_count, sharing, capacity, width)).reshape(
            experts, capacity, width
        )
        received = lax.all_to_all(outgoing, "expert", split_axis=0, concat_axis=0, tiled=True)
        owned = jnp.zeros((), jnp.int32)
        return (received.reshape(slot_count, width), owned)

    def finish_rows(received, compute):
        width = received.shape[1]
        result_list = compute(received)
        returned = lax.all_to_all(
            result_list.reshape(experts, capacity, width),
            "expert",
            split_axis=0,
            concat_axis=0,
            tiled=True,
        )
        gathered = jnp.sum(
            returned.reshape(exp_count, sharing, capacity, width).astype(jnp.float32), axis=1
        )
        return gathered.reshape(exp_count * capacity, width)

    fwd_rows, fwd_owned = send_rows(arrived, fwd_place)
    fwd_back = finish_rows(fwd_rows, forward_rows)
    bwd_rows, bwd_owned = send_rows(cotangent, bwd_place)
    bwd_back = finish_rows(bwd_rows, backward_rows)
    fwd_next = arrived.astype(jnp.float32) + jnp.dot(
        fwd_weigh, fwd_back, precision=lax.Precision.HIGHEST
    )
    bwd_next = cotangent.astype(jnp.float32) + jnp.dot(
        bwd_weigh, bwd_back, precision=lax.Precision.HIGHEST
    )
    totals = lax.psum(fwd_count + bwd_count, ("expert", "dp"))
    expert_load = lax.dynamic_slice_in_dim(totals, lax.axis_index("expert") // sharing, 1)[0]
    return (
        fwd_next.astype(jnp.bfloat16)[None],
        bwd_next.astype(jnp.bfloat16)[None],
        expert_load.reshape(1, 1),
    )


def solution(mesh):
    in_specs = (
        P("section", ("expert", "dp"), None),
        P("section", ("expert", "dp"), None),
        P("section", ("expert", "dp"), None),
        P("section", ("expert", "dp"), None),
        P("section", ("expert", "dp"), None),
        P("section", ("expert", "dp"), None),
        P("section", "dp", None, None, "expert"),
        P("section", None, "expert"),
        P("section", None, "expert"),
        P("section", "expert", None),
    )
    out_specs = (
        P("section", ("expert", "dp"), None),
        P("section", ("expert", "dp"), None),
        P("section", "expert"),
    )
    return jax.shard_map(shards, mesh=mesh, in_specs=in_specs, out_specs=out_specs, check_vma=False)
```

```python
import functools

import jax
import jax.numpy as jnp
from jax import lax
from jax.experimental import pallas as pl
from jax.experimental.pallas import tpu as pltpu
from jax.sharding import PartitionSpec as P

MESH = pl.DeviceIdType.MESH
LEFT, RIGHT = 0, 1
FWD, BWD = 0, 1
GATHER_CHUNKS = 4
RETURN_CHUNKS = 4


def from_behind(array, axis, by):
    length = lax.axis_size(axis)
    return lax.ppermute(array, axis, [(i, (i + by) % length) for i in range(length)])


def slot_tables(routes, probs, exp_count, capacity):
    slot_count = exp_count * capacity
    flat_routes = routes.reshape(-1)
    onehot = (flat_routes[:, None] == jnp.arange(exp_count, dtype=jnp.int32)[None, :]).astype(
        jnp.int32
    )
    before = jnp.cumsum(onehot, axis=0) - onehot
    position = jnp.sum(before * onehot, axis=1)
    slot_ids = flat_routes * capacity + position
    matches = (slot_ids[:, None] == jnp.arange(slot_count, dtype=jnp.int32)[None, :]).astype(
        jnp.float32
    )
    matches = matches.reshape(routes.shape[0], routes.shape[1], slot_count)
    placing = jnp.sum(matches, axis=1)
    weighing = jnp.sum(matches * probs[:, :, None], axis=1)
    counted = jnp.sum(onehot, axis=0)
    return (placing, weighing, counted)


def cuts(width, wanted, small_first):
    unit = 256
    count = width // unit
    pieces = min(wanted, count)
    sizes = [count // pieces + (1 if i < count % pieces else 0) for i in range(pieces)]
    if small_first:
        sizes = sizes[::-1]
    starts = [sum(sizes[:i]) for i in range(pieces)]
    return [pl.ds(a * unit, b * unit) for a, b in zip(starts, sizes)]


def relay_kernel(
    size,
    x_hbm,
    cot_hbm,
    f_routes,
    b_routes,
    f_probs,
    b_probs,
    saved_hbm,
    gate_hbm,
    up_hbm,
    down_hbm,
    f_out,
    b_out,
    load_out,
    gate_w,
    up_w,
    down_w,
    saved,
    x_own,
    rows_all,
    meta,
    from_right,
    from_left,
    going,
    part,
    hidden_acc,
    grad_acc,
    mid,
    w_sem,
    shift_send,
    shift_recv,
    meta_send,
    meta_recv,
    g_send,
    g_recv,
    r_send,
    r_recv,
):
    n, n_dp, n_sec, sharing, cap, rows = size
    group = n * n_dp
    width = cot_hbm.shape[1]
    me = lax.axis_index("expert")
    dp = lax.axis_index("dp")
    sec = lax.axis_index("section")
    lin = me * n_dp + dp
    g_cuts = cuts(width, GATHER_CHUNKS, False)
    r_cuts = cuts(width, RETURN_CHUNKS, True)
    contract_last = (((1,), (1,)), ((), ()))

    def place(block):
        return pl.ds(pl.multiple_of(block * rows, rows), rows)

    own_rows = [
        pltpu.make_async_copy(x_hbm, x_own, w_sem.at[4]),
        pltpu.make_async_copy(cot_hbm, rows_all.at[BWD, place(me), :], w_sem.at[5]),
    ]
    for load in own_rows:
        load.start()
    loads = [
        pltpu.make_async_copy(down_hbm, down_w, w_sem.at[0]),
        pltpu.make_async_copy(saved_hbm, saved, w_sem.at[1]),
        pltpu.make_async_copy(gate_hbm, gate_w, w_sem.at[2]),
        pltpu.make_async_copy(up_hbm, up_w, w_sem.at[3]),
    ]
    for load in loads[:2]:
        load.start()

    barrier = pltpu.get_barrier_semaphore()

    def peer(off):
        other = lax.rem(lin + off, group)
        return {"expert": lax.div(other, n_dp), "dp": lax.rem(other, n_dp)}

    for off in range(1, group):
        pl.semaphore_signal(barrier, inc=1, device_id=peer(off), device_id_type=MESH)
    pl.semaphore_signal(
        barrier,
        inc=1,
        device_id={"section": lax.rem(sec + n_sec - 1, n_sec)},
        device_id_type=MESH,
    )

    at_row = lax.broadcasted_iota(jnp.int32, (rows, rows), 0)
    at_col = lax.broadcasted_iota(jnp.int32, (rows, rows), 1)
    eye = at_row == at_col

    def column(line):
        spread = jnp.where(eye, jnp.broadcast_to(line, (rows, rows)), 0.0)
        return jnp.sum(spread, axis=1, keepdims=True)

    meta[lin] = jnp.zeros(meta.shape[1:], jnp.float32)
    for span, routes in ((FWD, f_routes), (BWD, b_routes)):
        named_row = routes[...].astype(jnp.float32)
        named = column(named_row)
        earlier = jnp.where((named == named_row) & (at_row < at_col), 1.0, 0.0)
        slot = named_row * cap + jnp.sum(earlier, axis=0, keepdims=True)
        meta[lin, span : span + 1, 0:rows] = slot
    pl.semaphore_wait(barrier, group)

    def gather_copy(span, way, hop, chunk):
        block = me - (hop - 1) if way == RIGHT else me + (hop - 1)
        there = me + 1 if way == RIGHT else me - 1
        piece = rows_all.at[span, place(block), g_cuts[chunk]]
        return pltpu.make_async_remote_copy(
            src_ref=piece,
            dst_ref=piece,
            send_sem=g_send.at[span, way, hop - 1, chunk],
            recv_sem=g_recv.at[span, way, hop - 1, chunk],
            device_id={"expert": there},
            device_id_type=MESH,
        )

    def gather_sends(way, hop):
        if way == RIGHT:
            return (me >= hop - 1) & (me < n - 1)
        return (me <= n - hop) & (me > 0)

    def gather_wait(span, way, hop, chunk):
        block = me - hop if way == RIGHT else me + hop
        there = me - 1 if way == RIGHT else me + 1
        piece = rows_all.at[span, place(block), g_cuts[chunk]]
        pltpu.make_async_remote_copy(
            src_ref=piece,
            dst_ref=piece,
            send_sem=g_send.at[span, way, hop - 1, chunk],
            recv_sem=g_recv.at[span, way, hop - 1, chunk],
            device_id={"expert": there},
            device_id_type=MESH,
        ).wait_recv()

    def gather_start(span, hop, chunk):
        for way in (LEFT, RIGHT):

            @pl.when(gather_sends(way, hop))
            def _():
                gather_copy(span, way, hop, chunk).start()

    inner = (me > 0) & (me < n - 1)

    def gather_step(span, hop, chunk):
        for way in (LEFT, RIGHT):
            there = me >= hop if way == RIGHT else me + hop < n

            @pl.when(there & inner)
            def _():
                gather_wait(span, way, hop, chunk)

            if hop < n - 1:

                @pl.when(gather_sends(way, hop + 1))
                def _():
                    gather_copy(span, way, hop + 1, chunk).start()

    def gather_rest(span, chunk):
        @pl.when(me == 0)
        def _():
            for hop in range(1, n):
                gather_wait(span, LEFT, hop, chunk)

        @pl.when(me == n - 1)
        def _():
            for hop in range(1, n):
                gather_wait(span, RIGHT, hop, chunk)

    def return_copy(span, way, block, chunk):
        landing = from_left if way == RIGHT else from_right
        there = me + 1 if way == RIGHT else me - 1
        spot = pl.ds(block * rows, rows)
        return pltpu.make_async_remote_copy(
            src_ref=going.at[span, spot, r_cuts[chunk]],
            dst_ref=landing.at[span, spot, r_cuts[chunk]],
            send_sem=r_send.at[span, way, block, chunk],
            recv_sem=r_recv.at[span, way, block, chunk],
            device_id={"expert": there},
            device_id_type=MESH,
        )

    def return_wait(span, way, block, chunk):
        landing = from_left if way == RIGHT else from_right
        there = me - 1 if way == RIGHT else me + 1
        piece = landing.at[span, place(block), r_cuts[chunk]]
        pltpu.make_async_remote_copy(
            src_ref=piece,
            dst_ref=piece,
            send_sem=r_send.at[span, way, block, chunk],
            recv_sem=r_recv.at[span, way, block, chunk],
            device_id={"expert": there},
            device_id_type=MESH,
        ).wait_recv()

    def return_step(span, hop, chunk):
        for way in (LEFT, RIGHT):
            at = n - 1 - hop if way == LEFT else hop
            blocks = range(at) if way == LEFT else range(n - 1, at, -1)
            landing = from_left if way == RIGHT else from_right

            @pl.when(me == at)
            def _():
                for block in blocks:
                    spot = pl.ds(block * rows, rows)
                    total = part[span, spot, r_cuts[chunk]]
                    if hop > 0:
                        return_wait(span, way, block, chunk)
                        total = total + landing[span, spot, r_cuts[chunk]].astype(jnp.float32)
                    going[span, spot, r_cuts[chunk]] = total.astype(jnp.bfloat16)
                    return_copy(span, way, block, chunk).start()

    def finish(span, chunk, base, probs, out):
        spot = place(me)
        for way in (LEFT, RIGHT):
            landing = from_left if way == RIGHT else from_right
            there = me > 0 if way == RIGHT else me < n - 1

            @pl.when(there)
            def _():
                return_wait(span, way, me, chunk)
                part[span, spot, r_cuts[chunk]] += landing[span, spot, r_cuts[chunk]].astype(
                    jnp.float32
                )

        out[:, r_cuts[chunk]] = (
            base(r_cuts[chunk]).astype(jnp.float32)
            + column(probs[...]) * part[span, spot, r_cuts[chunk]]
        )

    def meta_copy(off):
        return pltpu.make_async_remote_copy(
            src_ref=meta.at[lin],
            dst_ref=meta.at[lin],
            send_sem=meta_send.at[off],
            recv_sem=meta_recv.at[off],
            device_id=peer(off),
            device_id_type=MESH,
        )

    def meta_wait(off):
        other = meta.at[lax.rem(lin + group - off, group)]
        pltpu.make_async_remote_copy(
            src_ref=other,
            dst_ref=other,
            send_sem=meta_send.at[off],
            recv_sem=meta_recv.at[off],
            device_id=peer(group - off),
            device_id_type=MESH,
        ).wait_recv()

    def shift_copy(chunk):
        return pltpu.make_async_remote_copy(
            src_ref=x_own.at[:, g_cuts[chunk]],
            dst_ref=rows_all.at[FWD, place(me), g_cuts[chunk]],
            send_sem=shift_send.at[chunk],
            recv_sem=shift_recv.at[chunk],
            device_id={"section": lax.rem(sec + 1, n_sec)},
            device_id_type=MESH,
        )

    own_rows[0].wait()
    for chunk in range(len(g_cuts)):
        shift_copy(chunk).start()
    own_rows[1].wait()
    for chunk in range(len(g_cuts)):
        gather_start(BWD, 1, chunk)
    for load in loads[2:]:
        load.start()
    for off in range(1, group):
        meta_copy(off).start()

    for hop in range(1, n - 1):
        for chunk in range(len(g_cuts)):
            gather_step(BWD, hop, chunk)
        if hop == n - 2:
            for chunk in range(len(g_cuts)):
                shift_copy(chunk).wait_recv()
                gather_start(FWD, 1, chunk)
            for off in range(1, group):
                meta_wait(off)
            first = (lax.div(me, sharing) * cap).astype(jnp.float32)
            owned = jnp.zeros((2, rows), jnp.float32)
            for other in range(group):
                slots = meta[other, 0:2, 0:rows] - first
                owned = owned + jnp.where((slots >= 0.0) & (slots < cap), 1.0, 0.0)
            owned = jnp.sum(jnp.sum(owned, axis=1, keepdims=True), axis=0, keepdims=True)
            load_out[...] = owned.astype(jnp.int32)

            def slots_of(span, block):
                line = meta[block * n_dp + dp, span : span + 1, 0:rows] - first
                return column(line)

            lanes = lax.broadcasted_iota(jnp.int32, (rows, n * cap), 1).astype(jnp.float32)
            taken = []
            for block in range(n):
                slots = slots_of(BWD, block)
                hit = (slots >= 0.0) & (slots < cap) & (lanes == slots + block * cap)
                taken.append(jnp.where(hit, 1.0, 0.0))
            taken = jnp.concatenate(taken, axis=0).astype(jnp.bfloat16)
            kept = []
            for block in range(n):
                slots = slots_of(FWD, block)
                kept.append(jnp.where((slots >= 0.0) & (slots < cap), 1.0, 0.0))
            kept = jnp.concatenate(kept, axis=0) > 0.5
            loads[1].wait()
            stored = saved[...].astype(jnp.float32)
            saved_gate = jnp.dot(
                taken, stored[:, 0, :].astype(jnp.bfloat16), preferred_element_type=jnp.float32
            )
            saved_up = jnp.dot(
                taken, stored[:, 1, :].astype(jnp.bfloat16), preferred_element_type=jnp.float32
            )
            sigma = jax.nn.sigmoid(saved_gate)
            hidden_acc[0] = saved_up * sigma * (1.0 + saved_gate * (1.0 - sigma))
            hidden_acc[1] = saved_gate * sigma

    loads[0].wait()
    for chunk, cut in enumerate(g_cuts):
        gather_rest(BWD, chunk)
        term = lax.dot_general(
            down_w[:, cut],
            rows_all[BWD, :, cut],
            contract_last,
            preferred_element_type=jnp.float32,
        )
        if chunk == 0:
            grad_acc[...] = term
        else:
            grad_acc[...] += term
    grad_hidden = grad_acc[...].T
    mid[0] = (grad_hidden * hidden_acc[0]).astype(jnp.bfloat16)
    mid[1] = (grad_hidden * hidden_acc[1]).astype(jnp.bfloat16)

    loads[2].wait()
    loads[3].wait()

    def bwd_part(chunk):
        cut = r_cuts[chunk]
        turned = lax.dot_general(
            gate_w[cut, :], mid[0], contract_last, preferred_element_type=jnp.float32
        ) + lax.dot_general(
            up_w[cut, :], mid[1], contract_last, preferred_element_type=jnp.float32
        )
        part[BWD, :, cut] = turned.T

    r_count, g_count = len(r_cuts), len(g_cuts)
    for chunk in range(max(r_count, g_count)):
        if chunk < r_count:
            bwd_part(chunk)
            return_step(BWD, 0, chunk)
        if chunk < g_count:
            gather_step(FWD, 1, chunk)
    for hop in range(1, n - 2):
        for chunk in range(max(r_count, g_count)):
            if chunk < g_count:
                gather_step(FWD, hop + 1, chunk)
            if chunk < r_count:
                return_step(BWD, hop, chunk)

    for chunk, cut in enumerate(g_cuts):
        gather_rest(FWD, chunk)
        for at, weights in ((0, gate_w), (1, up_w)):
            term = jnp.dot(
                rows_all[FWD, :, cut], weights[cut, :], preferred_element_type=jnp.float32
            )
            if chunk == 0:
                hidden_acc[at] = term
            else:
                hidden_acc[at] += term
        if chunk < r_count:
            return_step(BWD, n - 2, chunk)
    for chunk in range(g_count, r_count):
        return_step(BWD, n - 2, chunk)
    activated = jax.nn.silu(hidden_acc[0]) * hidden_acc[1]
    mid[0] = jnp.where(kept, activated, 0.0).astype(jnp.bfloat16)

    for chunk in range(r_count):
        cut = r_cuts[chunk]
        part[FWD, :, cut] = jnp.dot(mid[0], down_w[:, cut], preferred_element_type=jnp.float32)
        return_step(FWD, 0, chunk)
    for hop in range(1, n - 1):
        for chunk in range(r_count):
            return_step(FWD, hop, chunk)
    for chunk in range(r_count):
        finish(BWD, chunk, lambda cut: rows_all[BWD, place(me), cut], b_probs, b_out)
    for chunk in range(r_count):
        finish(FWD, chunk, lambda cut: rows_all[FWD, place(me), cut], f_probs, f_out)

    for chunk in range(len(g_cuts)):
        shift_copy(chunk).wait_send()
    for off in range(1, group):
        meta_copy(off).wait_send()
    for span in (BWD, FWD):
        for way in (LEFT, RIGHT):
            for hop in range(1, n):

                @pl.when(gather_sends(way, hop))
                def _():
                    for chunk in range(len(g_cuts)):
                        gather_copy(span, way, hop, chunk).wait_send()

            for block in range(n):

                @pl.when(me > block if way == LEFT else me < block)
                def _():
                    for chunk in range(r_count):
                        return_copy(span, way, block, chunk).wait_send()


def relay_fits(fwd_sent, top_count, capacity):
    rows, width = fwd_sent.shape[1:]
    return (
        top_count == 1
        and capacity == rows
        and rows % 16 == 0
        and rows <= 128
        and width % 256 == 0
        and lax.axis_size("expert") > 2
        and lax.axis_size("section") > 1
    )


def relay(
    fwd_sent,
    fwd_routes,
    fwd_probs,
    backward_cotangent,
    bwd_routes,
    bwd_probs,
    saved_pre,
    w_gate,
    w_up,
    w_down,
    *,
    sharing,
    capacity,
):
    n, n_dp, n_sec = (lax.axis_size(name) for name in ("expert", "dp", "section"))
    rows, width = fwd_sent.shape[1:]
    hidden = w_gate.shape[2]
    tokens = n * rows
    bf16, f32 = jnp.bfloat16, jnp.float32
    group = n * n_dp
    g_count = len(cuts(width, GATHER_CHUNKS, False))
    r_count = len(cuts(width, RETURN_CHUNKS, True))
    vmem = pl.BlockSpec(memory_space=pltpu.VMEM)
    hbm = pl.BlockSpec(memory_space=pl.ANY)
    f_next, b_next, load = pl.pallas_call(
        functools.partial(relay_kernel, (n, n_dp, n_sec, sharing, capacity, rows)),
        out_shape=(
            jax.ShapeDtypeStruct((rows, width), f32),
            jax.ShapeDtypeStruct((rows, width), f32),
            jax.ShapeDtypeStruct((1, 1), jnp.int32),
        ),
        in_specs=[hbm] * 2 + [vmem] * 4 + [hbm] * 4,
        out_specs=(vmem, vmem, vmem),
        scratch_shapes=[
            pltpu.VMEM((width, hidden), bf16),
            pltpu.VMEM((width, hidden), bf16),
            pltpu.VMEM((hidden, width), bf16),
            pltpu.VMEM(saved_pre.shape[2:], bf16),
            pltpu.VMEM((rows, width), bf16),
            pltpu.VMEM((2, tokens, width), bf16),
            pltpu.VMEM((group, 8, 128), f32),
            pltpu.VMEM((2, tokens, width), bf16),
            pltpu.VMEM((2, tokens, width), bf16),
            pltpu.VMEM((2, tokens, width), bf16),
            pltpu.VMEM((2, tokens, width), f32),
            pltpu.VMEM((2, tokens, hidden), f32),
            pltpu.VMEM((hidden, tokens), f32),
            pltpu.VMEM((2, tokens, hidden), bf16),
            pltpu.SemaphoreType.DMA((6,)),
            pltpu.SemaphoreType.DMA((g_count,)),
            pltpu.SemaphoreType.DMA((g_count,)),
            pltpu.SemaphoreType.DMA((group,)),
            pltpu.SemaphoreType.DMA((group,)),
            pltpu.SemaphoreType.DMA((2, 2, n - 1, g_count)),
            pltpu.SemaphoreType.DMA((2, 2, n - 1, g_count)),
            pltpu.SemaphoreType.DMA((2, 2, n, r_count)),
            pltpu.SemaphoreType.DMA((2, 2, n, r_count)),
        ],
        compiler_params=pltpu.CompilerParams(
            collective_id=0, has_side_effects=True, vmem_limit_bytes=60 * 1024 * 1024
        ),
        cost_estimate=pl.CostEstimate(
            flops=12 * tokens * width * hidden,
            bytes_accessed=6 * width * hidden,
            transcendentals=2 * tokens * hidden,
        ),
    )(
        fwd_sent[0],
        backward_cotangent[0],
        fwd_routes.reshape(1, rows),
        bwd_routes.reshape(1, rows),
        fwd_probs.reshape(1, rows),
        bwd_probs.reshape(1, rows),
        saved_pre[0, 0],
        w_gate[0],
        w_up[0],
        w_down[0],
    )
    return f_next.astype(bf16)[None], b_next.astype(bf16)[None], load


def shards(
    fwd_sent,
    fwd_routes,
    fwd_probs,
    backward_cotangent,
    bwd_routes,
    bwd_probs,
    saved_pre,
    w_gate,
    w_up,
    w_down,
):
    experts = lax.axis_size("expert")
    sharing = min(4, experts // 2)
    exp_count = experts // sharing
    token_rows = fwd_sent.shape[1]
    top_count = fwd_routes.shape[2]
    capacity = min(token_rows, max(2, 2 * token_rows * top_count // exp_count))
    slot_count = experts * capacity
    if relay_fits(fwd_sent, top_count, capacity):
        return relay(
            fwd_sent,
            fwd_routes,
            fwd_probs,
            backward_cotangent,
            bwd_routes,
            bwd_probs,
            saved_pre,
            w_gate,
            w_up,
            w_down,
            sharing=sharing,
            capacity=capacity,
        )
    arrived = from_behind(fwd_sent, "section", 1)[0]
    gate_mat = w_gate[0]
    up_mat = w_up[0]
    down_mat = w_down[0]
    stored = saved_pre[0, 0]
    cotangent = backward_cotangent[0]
    fwd_place, fwd_weigh, fwd_count = slot_tables(fwd_routes[0], fwd_probs[0], exp_count, capacity)
    bwd_place, bwd_weigh, bwd_count = slot_tables(bwd_routes[0], bwd_probs[0], exp_count, capacity)

    def forward_rows(slot_rows):
        gate_pre = jnp.dot(slot_rows, gate_mat, preferred_element_type=jnp.float32)
        up_pre = jnp.dot(slot_rows, up_mat, preferred_element_type=jnp.float32)
        hidden_state = (jax.nn.silu(gate_pre) * up_pre).astype(jnp.bfloat16)
        return jnp.dot(hidden_state, down_mat, preferred_element_type=jnp.float32).astype(
            jnp.bfloat16
        )

    def backward_rows(slot_rows):
        contract = (((1,), (1,)), ((), ()))
        grad_hidden = lax.dot_general(
            slot_rows, down_mat, contract, preferred_element_type=jnp.float32
        )
        saved_gate = stored[:, 0].astype(jnp.float32)
        saved_up = stored[:, 1].astype(jnp.float32)
        sigma = jax.nn.sigmoid(saved_gate)
        grad_gate = (grad_hidden * saved_up * sigma * (1.0 + saved_gate * (1.0 - sigma))).astype(
            jnp.bfloat16
        )
        grad_up = (grad_hidden * saved_gate * sigma).astype(jnp.bfloat16)
        summed = lax.dot_general(grad_gate, gate_mat, contract, preferred_element_type=jnp.float32)
        summed = summed + lax.dot_general(
            grad_up, up_mat, contract, preferred_element_type=jnp.float32
        )
        return summed.astype(jnp.bfloat16)

    def send_rows(tokens, placing):
        width = tokens.shape[1]
        outgoing = jnp.dot(
            placing.T.astype(jnp.bfloat16), tokens, preferred_element_type=jnp.float32
        )
        outgoing = outgoing.astype(jnp.bfloat16).reshape(exp_count, 1, capacity, width)
        outgoing = jnp.broadcast_to(outgoing, (exp_count, sharing, capacity, width)).reshape(
            experts, capacity, width
        )
        received = lax.all_to_all(outgoing, "expert", split_axis=0, concat_axis=0, tiled=True)
        owned = jnp.zeros((), jnp.int32)
        return (received.reshape(slot_count, width), owned)

    def finish_rows(received, compute):
        width = received.shape[1]
        result_list = compute(received)
        returned = lax.all_to_all(
            result_list.reshape(experts, capacity, width),
            "expert",
            split_axis=0,
            concat_axis=0,
            tiled=True,
        )
        gathered = jnp.sum(
            returned.reshape(exp_count, sharing, capacity, width).astype(jnp.float32), axis=1
        )
        return gathered.reshape(exp_count * capacity, width)

    fwd_rows, fwd_owned = send_rows(arrived, fwd_place)
    fwd_back = finish_rows(fwd_rows, forward_rows)
    bwd_rows, bwd_owned = send_rows(cotangent, bwd_place)
    bwd_back = finish_rows(bwd_rows, backward_rows)
    fwd_next = arrived.astype(jnp.float32) + jnp.dot(
        fwd_weigh, fwd_back, precision=lax.Precision.HIGHEST
    )
    bwd_next = cotangent.astype(jnp.float32) + jnp.dot(
        bwd_weigh, bwd_back, precision=lax.Precision.HIGHEST
    )
    totals = lax.psum(fwd_count + bwd_count, ("expert", "dp"))
    expert_load = lax.dynamic_slice_in_dim(totals, lax.axis_index("expert") // sharing, 1)[0]
    return (
        fwd_next.astype(jnp.bfloat16)[None],
        bwd_next.astype(jnp.bfloat16)[None],
        expert_load.reshape(1, 1),
    )


def solution(mesh):
    in_specs = (
        P("section", ("expert", "dp"), None),
        P("section", ("expert", "dp"), None),
        P("section", ("expert", "dp"), None),
        P("section", ("expert", "dp"), None),
        P("section", ("expert", "dp"), None),
        P("section", ("expert", "dp"), None),
        P("section", "dp", None, None, "expert"),
        P("section", None, "expert"),
        P("section", None, "expert"),
        P("section", "expert", None),
    )
    out_specs = (
        P("section", ("expert", "dp"), None),
        P("section", ("expert", "dp"), None),
        P("section", "expert"),
    )
    return jax.shard_map(shards, mesh=mesh, in_specs=in_specs, out_specs=out_specs, check_vma=False)
```

```python
import functools

import jax
import jax.numpy as jnp
from jax import lax
from jax.experimental import pallas as pl
from jax.experimental.pallas import tpu as pltpu
from jax.sharding import PartitionSpec as P

MESH = pl.DeviceIdType.MESH
LEFT, RIGHT = 0, 1
FWD, BWD = 0, 1
GATHER_CHUNKS = 4
RETURN_CHUNKS = 4


def from_behind(array, axis, by):
    length = lax.axis_size(axis)
    return lax.ppermute(array, axis, [(i, (i + by) % length) for i in range(length)])


def slot_tables(routes, probs, exp_count, capacity):
    slot_count = exp_count * capacity
    flat_routes = routes.reshape(-1)
    onehot = (flat_routes[:, None] == jnp.arange(exp_count, dtype=jnp.int32)[None, :]).astype(
        jnp.int32
    )
    before = jnp.cumsum(onehot, axis=0) - onehot
    position = jnp.sum(before * onehot, axis=1)
    slot_ids = flat_routes * capacity + position
    matches = (slot_ids[:, None] == jnp.arange(slot_count, dtype=jnp.int32)[None, :]).astype(
        jnp.float32
    )
    matches = matches.reshape(routes.shape[0], routes.shape[1], slot_count)
    placing = jnp.sum(matches, axis=1)
    weighing = jnp.sum(matches * probs[:, :, None], axis=1)
    counted = jnp.sum(onehot, axis=0)
    return (placing, weighing, counted)


def cuts(width, wanted, small_first):
    unit = 256
    count = width // unit
    pieces = min(wanted, count)
    sizes = [count // pieces + (1 if i < count % pieces else 0) for i in range(pieces)]
    if small_first:
        sizes = sizes[::-1]
    starts = [sum(sizes[:i]) for i in range(pieces)]
    return [pl.ds(a * unit, b * unit) for a, b in zip(starts, sizes)]


def relay_kernel(
    size,
    x_hbm,
    cot_hbm,
    f_routes,
    b_routes,
    f_probs,
    b_probs,
    saved_hbm,
    gate_hbm,
    up_hbm,
    down_hbm,
    f_out,
    b_out,
    load_out,
    gate_w,
    up_w,
    down_w,
    saved,
    x_own,
    rows_all,
    meta,
    from_right,
    from_left,
    going,
    part,
    hidden_acc,
    grad_acc,
    mid,
    w_sem,
    shift_send,
    shift_recv,
    meta_send,
    meta_recv,
    g_send,
    g_recv,
    r_send,
    r_recv,
):
    n, n_dp, n_sec, sharing, cap, rows = size
    group = n * n_dp
    width = cot_hbm.shape[1]
    me = lax.axis_index("expert")
    dp = lax.axis_index("dp")
    sec = lax.axis_index("section")
    lin = me * n_dp + dp
    g_cuts = cuts(width, GATHER_CHUNKS, False)
    r_cuts = cuts(width, RETURN_CHUNKS, True)
    contract_last = (((1,), (1,)), ((), ()))

    def place(block):
        return pl.ds(pl.multiple_of(block * rows, rows), rows)

    own_rows = [
        pltpu.make_async_copy(x_hbm, x_own, w_sem.at[4]),
        pltpu.make_async_copy(cot_hbm, rows_all.at[BWD, place(me), :], w_sem.at[5]),
    ]
    for load in own_rows:
        load.start()
    loads = [
        pltpu.make_async_copy(down_hbm, down_w, w_sem.at[0]),
        pltpu.make_async_copy(saved_hbm, saved, w_sem.at[1]),
        pltpu.make_async_copy(gate_hbm, gate_w, w_sem.at[2]),
        pltpu.make_async_copy(up_hbm, up_w, w_sem.at[3]),
    ]
    for load in loads[:2]:
        load.start()

    barrier = pltpu.get_barrier_semaphore()

    def peer(off):
        other = lax.rem(lin + off, group)
        return {"expert": lax.div(other, n_dp), "dp": lax.rem(other, n_dp)}

    for off in range(1, group):
        pl.semaphore_signal(barrier, inc=1, device_id=peer(off), device_id_type=MESH)
    pl.semaphore_signal(
        barrier,
        inc=1,
        device_id={"section": lax.rem(sec + n_sec - 1, n_sec)},
        device_id_type=MESH,
    )

    at_row = lax.broadcasted_iota(jnp.int32, (rows, rows), 0)
    at_col = lax.broadcasted_iota(jnp.int32, (rows, rows), 1)
    eye = at_row == at_col

    def column(line):
        spread = jnp.where(eye, jnp.broadcast_to(line, (rows, rows)), 0.0)
        return jnp.sum(spread, axis=1, keepdims=True)

    meta[lin] = jnp.zeros(meta.shape[1:], jnp.float32)
    for span, routes in ((FWD, f_routes), (BWD, b_routes)):
        named_row = routes[...].astype(jnp.float32)
        named = column(named_row)
        earlier = jnp.where((named == named_row) & (at_row < at_col), 1.0, 0.0)
        slot = named_row * cap + jnp.sum(earlier, axis=0, keepdims=True)
        meta[lin, span : span + 1, 0:rows] = slot
    pl.semaphore_wait(barrier, group)

    def gather_copy(span, way, hop, chunk):
        block = me - (hop - 1) if way == RIGHT else me + (hop - 1)
        there = me + 1 if way == RIGHT else me - 1
        piece = rows_all.at[span, place(block), g_cuts[chunk]]
        return pltpu.make_async_remote_copy(
            src_ref=piece,
            dst_ref=piece,
            send_sem=g_send.at[span, way, hop - 1, chunk],
            recv_sem=g_recv.at[span, way, hop - 1, chunk],
            device_id={"expert": there},
            device_id_type=MESH,
        )

    def gather_sends(way, hop):
        if way == RIGHT:
            return (me >= hop - 1) & (me < n - 1)
        return (me <= n - hop) & (me > 0)

    def gather_wait(span, way, hop, chunk):
        block = me - hop if way == RIGHT else me + hop
        there = me - 1 if way == RIGHT else me + 1
        piece = rows_all.at[span, place(block), g_cuts[chunk]]
        pltpu.make_async_remote_copy(
            src_ref=piece,
            dst_ref=piece,
            send_sem=g_send.at[span, way, hop - 1, chunk],
            recv_sem=g_recv.at[span, way, hop - 1, chunk],
            device_id={"expert": there},
            device_id_type=MESH,
        ).wait_recv()

    def gather_start(span, hop, chunk):
        for way in (LEFT, RIGHT):

            @pl.when(gather_sends(way, hop))
            def _():
                gather_copy(span, way, hop, chunk).start()

    inner = (me > 0) & (me < n - 1)

    def gather_step(span, hop, chunk):
        for way in (LEFT, RIGHT):
            there = me >= hop if way == RIGHT else me + hop < n

            @pl.when(there & inner)
            def _():
                gather_wait(span, way, hop, chunk)

            if hop < n - 1:

                @pl.when(gather_sends(way, hop + 1))
                def _():
                    gather_copy(span, way, hop + 1, chunk).start()

    def gather_rest(span, chunk):
        @pl.when(me == 0)
        def _():
            for hop in range(1, n):
                gather_wait(span, LEFT, hop, chunk)

        @pl.when(me == n - 1)
        def _():
            for hop in range(1, n):
                gather_wait(span, RIGHT, hop, chunk)

    def return_copy(span, way, block, chunk):
        landing = from_left if way == RIGHT else from_right
        there = me + 1 if way == RIGHT else me - 1
        spot = pl.ds(block * rows, rows)
        return pltpu.make_async_remote_copy(
            src_ref=going.at[span, spot, r_cuts[chunk]],
            dst_ref=landing.at[span, spot, r_cuts[chunk]],
            send_sem=r_send.at[span, way, block, chunk],
            recv_sem=r_recv.at[span, way, block, chunk],
            device_id={"expert": there},
            device_id_type=MESH,
        )

    def return_wait(span, way, block, chunk):
        landing = from_left if way == RIGHT else from_right
        there = me - 1 if way == RIGHT else me + 1
        piece = landing.at[span, place(block), r_cuts[chunk]]
        pltpu.make_async_remote_copy(
            src_ref=piece,
            dst_ref=piece,
            send_sem=r_send.at[span, way, block, chunk],
            recv_sem=r_recv.at[span, way, block, chunk],
            device_id={"expert": there},
            device_id_type=MESH,
        ).wait_recv()

    def return_step(span, hop, chunk, nth):
        for way in (LEFT, RIGHT):
            at = n - 1 - hop if way == LEFT else hop
            block = nth if way == LEFT else n - 1 - nth
            landing = from_left if way == RIGHT else from_right

            @pl.when(me == at)
            def _():
                spot = pl.ds(block * rows, rows)
                total = part[span, spot, r_cuts[chunk]]
                if hop > 0:
                    return_wait(span, way, block, chunk)
                    total = total + landing[span, spot, r_cuts[chunk]].astype(jnp.float32)
                going[span, spot, r_cuts[chunk]] = total.astype(jnp.bfloat16)
                return_copy(span, way, block, chunk).start()

    onward = [(nth, hop) for nth in range(n - 1) for hop in range(1, n - 1 - nth)]

    def finish(span, chunk, base, probs, out):
        spot = place(me)
        for way in (LEFT, RIGHT):
            landing = from_left if way == RIGHT else from_right
            there = me > 0 if way == RIGHT else me < n - 1

            @pl.when(there)
            def _():
                return_wait(span, way, me, chunk)
                part[span, spot, r_cuts[chunk]] += landing[span, spot, r_cuts[chunk]].astype(
                    jnp.float32
                )

        out[:, r_cuts[chunk]] = (
            base(r_cuts[chunk]).astype(jnp.float32)
            + column(probs[...]) * part[span, spot, r_cuts[chunk]]
        )

    def meta_copy(off):
        return pltpu.make_async_remote_copy(
            src_ref=meta.at[lin],
            dst_ref=meta.at[lin],
            send_sem=meta_send.at[off],
            recv_sem=meta_recv.at[off],
            device_id=peer(off),
            device_id_type=MESH,
        )

    def meta_wait(off):
        other = meta.at[lax.rem(lin + group - off, group)]
        pltpu.make_async_remote_copy(
            src_ref=other,
            dst_ref=other,
            send_sem=meta_send.at[off],
            recv_sem=meta_recv.at[off],
            device_id=peer(group - off),
            device_id_type=MESH,
        ).wait_recv()

    def shift_copy(chunk):
        return pltpu.make_async_remote_copy(
            src_ref=x_own.at[:, g_cuts[chunk]],
            dst_ref=rows_all.at[FWD, place(me), g_cuts[chunk]],
            send_sem=shift_send.at[chunk],
            recv_sem=shift_recv.at[chunk],
            device_id={"section": lax.rem(sec + 1, n_sec)},
            device_id_type=MESH,
        )

    own_rows[0].wait()
    for chunk in range(len(g_cuts)):
        shift_copy(chunk).start()
    own_rows[1].wait()
    for chunk in range(len(g_cuts)):
        gather_start(BWD, 1, chunk)
    for load in loads[2:]:
        load.start()
    for off in range(1, group):
        meta_copy(off).start()

    for hop in range(1, n - 1):
        for chunk in range(len(g_cuts)):
            gather_step(BWD, hop, chunk)
        if hop == n - 2:
            for chunk in range(len(g_cuts)):
                shift_copy(chunk).wait_recv()
                gather_start(FWD, 1, chunk)
            for off in range(1, group):
                meta_wait(off)
            first = (lax.div(me, sharing) * cap).astype(jnp.float32)
            owned = jnp.zeros((2, rows), jnp.float32)
            for other in range(group):
                slots = meta[other, 0:2, 0:rows] - first
                owned = owned + jnp.where((slots >= 0.0) & (slots < cap), 1.0, 0.0)
            owned = jnp.sum(jnp.sum(owned, axis=1, keepdims=True), axis=0, keepdims=True)
            load_out[...] = owned.astype(jnp.int32)

            def slots_of(span, block):
                line = meta[block * n_dp + dp, span : span + 1, 0:rows] - first
                return column(line)

            lanes = lax.broadcasted_iota(jnp.int32, (rows, n * cap), 1).astype(jnp.float32)
            taken = []
            for block in range(n):
                slots = slots_of(BWD, block)
                hit = (slots >= 0.0) & (slots < cap) & (lanes == slots + block * cap)
                taken.append(jnp.where(hit, 1.0, 0.0))
            taken = jnp.concatenate(taken, axis=0).astype(jnp.bfloat16)
            kept = []
            for block in range(n):
                slots = slots_of(FWD, block)
                kept.append(jnp.where((slots >= 0.0) & (slots < cap), 1.0, 0.0))
            kept = jnp.concatenate(kept, axis=0) > 0.5
            loads[1].wait()
            stored = saved[...].astype(jnp.float32)
            saved_gate = jnp.dot(
                taken, stored[:, 0, :].astype(jnp.bfloat16), preferred_element_type=jnp.float32
            )
            saved_up = jnp.dot(
                taken, stored[:, 1, :].astype(jnp.bfloat16), preferred_element_type=jnp.float32
            )
            sigma = jax.nn.sigmoid(saved_gate)
            hidden_acc[0] = saved_up * sigma * (1.0 + saved_gate * (1.0 - sigma))
            hidden_acc[1] = saved_gate * sigma

    loads[0].wait()
    for chunk, cut in enumerate(g_cuts):
        gather_rest(BWD, chunk)
        term = lax.dot_general(
            down_w[:, cut],
            rows_all[BWD, :, cut],
            contract_last,
            preferred_element_type=jnp.float32,
        )
        if chunk == 0:
            grad_acc[...] = term
        else:
            grad_acc[...] += term
    grad_hidden = grad_acc[...].T
    mid[0] = (grad_hidden * hidden_acc[0]).astype(jnp.bfloat16)
    mid[1] = (grad_hidden * hidden_acc[1]).astype(jnp.bfloat16)

    loads[2].wait()
    loads[3].wait()

    def bwd_part(chunk):
        cut = r_cuts[chunk]
        turned = lax.dot_general(
            gate_w[cut, :], mid[0], contract_last, preferred_element_type=jnp.float32
        ) + lax.dot_general(
            up_w[cut, :], mid[1], contract_last, preferred_element_type=jnp.float32
        )
        part[BWD, :, cut] = turned.T

    r_count, g_count = len(r_cuts), len(g_cuts)
    for chunk in range(max(r_count, g_count)):
        if chunk < r_count:
            bwd_part(chunk)
            return_step(BWD, 0, chunk, 0)
        if chunk < g_count:
            gather_step(FWD, 1, chunk)
    for nth in range(1, n - 1):
        for chunk in range(r_count):
            return_step(BWD, 0, chunk, nth)
    for hop in range(1, n - 2):
        for chunk in range(max(r_count, g_count)):
            if chunk < g_count:
                gather_step(FWD, hop + 1, chunk)
            if chunk < r_count:
                return_step(BWD, hop, chunk, 0)
    late = [(nth, hop) for nth, hop in onward if nth > 0 or hop == n - 2]

    for chunk, cut in enumerate(g_cuts):
        gather_rest(FWD, chunk)
        for at, weights in ((0, gate_w), (1, up_w)):
            term = jnp.dot(
                rows_all[FWD, :, cut], weights[cut, :], preferred_element_type=jnp.float32
            )
            if chunk == 0:
                hidden_acc[at] = term
            else:
                hidden_acc[at] += term
        if chunk < r_count:
            for nth, hop in late:
                return_step(BWD, hop, chunk, nth)
    for chunk in range(g_count, r_count):
        for nth, hop in late:
            return_step(BWD, hop, chunk, nth)
    activated = jax.nn.silu(hidden_acc[0]) * hidden_acc[1]
    mid[0] = jnp.where(kept, activated, 0.0).astype(jnp.bfloat16)

    for chunk in range(r_count):
        cut = r_cuts[chunk]
        part[FWD, :, cut] = jnp.dot(mid[0], down_w[:, cut], preferred_element_type=jnp.float32)
        return_step(FWD, 0, chunk, 0)
    for nth in range(1, n - 1):
        for chunk in range(r_count):
            return_step(FWD, 0, chunk, nth)
    for nth, hop in onward:
        for chunk in range(r_count):
            return_step(FWD, hop, chunk, nth)
    for chunk in range(r_count):
        finish(BWD, chunk, lambda cut: rows_all[BWD, place(me), cut], b_probs, b_out)
    for chunk in range(r_count):
        finish(FWD, chunk, lambda cut: rows_all[FWD, place(me), cut], f_probs, f_out)

    for chunk in range(len(g_cuts)):
        shift_copy(chunk).wait_send()
    for off in range(1, group):
        meta_copy(off).wait_send()
    for span in (BWD, FWD):
        for way in (LEFT, RIGHT):
            for hop in range(1, n):

                @pl.when(gather_sends(way, hop))
                def _():
                    for chunk in range(len(g_cuts)):
                        gather_copy(span, way, hop, chunk).wait_send()

            for block in range(n):

                @pl.when(me > block if way == LEFT else me < block)
                def _():
                    for chunk in range(r_count):
                        return_copy(span, way, block, chunk).wait_send()


def relay_fits(fwd_sent, top_count, capacity):
    rows, width = fwd_sent.shape[1:]
    return (
        top_count == 1
        and capacity == rows
        and rows % 16 == 0
        and rows <= 128
        and width % 256 == 0
        and lax.axis_size("expert") > 2
        and lax.axis_size("section") > 1
    )


def relay(
    fwd_sent,
    fwd_routes,
    fwd_probs,
    backward_cotangent,
    bwd_routes,
    bwd_probs,
    saved_pre,
    w_gate,
    w_up,
    w_down,
    *,
    sharing,
    capacity,
):
    n, n_dp, n_sec = (lax.axis_size(name) for name in ("expert", "dp", "section"))
    rows, width = fwd_sent.shape[1:]
    hidden = w_gate.shape[2]
    tokens = n * rows
    bf16, f32 = jnp.bfloat16, jnp.float32
    group = n * n_dp
    g_count = len(cuts(width, GATHER_CHUNKS, False))
    r_count = len(cuts(width, RETURN_CHUNKS, True))
    vmem = pl.BlockSpec(memory_space=pltpu.VMEM)
    hbm = pl.BlockSpec(memory_space=pl.ANY)
    f_next, b_next, load = pl.pallas_call(
        functools.partial(relay_kernel, (n, n_dp, n_sec, sharing, capacity, rows)),
        out_shape=(
            jax.ShapeDtypeStruct((rows, width), f32),
            jax.ShapeDtypeStruct((rows, width), f32),
            jax.ShapeDtypeStruct((1, 1), jnp.int32),
        ),
        in_specs=[hbm] * 2 + [vmem] * 4 + [hbm] * 4,
        out_specs=(vmem, vmem, vmem),
        scratch_shapes=[
            pltpu.VMEM((width, hidden), bf16),
            pltpu.VMEM((width, hidden), bf16),
            pltpu.VMEM((hidden, width), bf16),
            pltpu.VMEM(saved_pre.shape[2:], bf16),
            pltpu.VMEM((rows, width), bf16),
            pltpu.VMEM((2, tokens, width), bf16),
            pltpu.VMEM((group, 8, 128), f32),
            pltpu.VMEM((2, tokens, width), bf16),
            pltpu.VMEM((2, tokens, width), bf16),
            pltpu.VMEM((2, tokens, width), bf16),
            pltpu.VMEM((2, tokens, width), f32),
            pltpu.VMEM((2, tokens, hidden), f32),
            pltpu.VMEM((hidden, tokens), f32),
            pltpu.VMEM((2, tokens, hidden), bf16),
            pltpu.SemaphoreType.DMA((6,)),
            pltpu.SemaphoreType.DMA((g_count,)),
            pltpu.SemaphoreType.DMA((g_count,)),
            pltpu.SemaphoreType.DMA((group,)),
            pltpu.SemaphoreType.DMA((group,)),
            pltpu.SemaphoreType.DMA((2, 2, n - 1, g_count)),
            pltpu.SemaphoreType.DMA((2, 2, n - 1, g_count)),
            pltpu.SemaphoreType.DMA((2, 2, n, r_count)),
            pltpu.SemaphoreType.DMA((2, 2, n, r_count)),
        ],
        compiler_params=pltpu.CompilerParams(
            collective_id=0, has_side_effects=True, vmem_limit_bytes=60 * 1024 * 1024
        ),
        cost_estimate=pl.CostEstimate(
            flops=12 * tokens * width * hidden,
            bytes_accessed=6 * width * hidden,
            transcendentals=2 * tokens * hidden,
        ),
    )(
        fwd_sent[0],
        backward_cotangent[0],
        fwd_routes.reshape(1, rows),
        bwd_routes.reshape(1, rows),
        fwd_probs.reshape(1, rows),
        bwd_probs.reshape(1, rows),
        saved_pre[0, 0],
        w_gate[0],
        w_up[0],
        w_down[0],
    )
    return f_next.astype(bf16)[None], b_next.astype(bf16)[None], load


def shards(
    fwd_sent,
    fwd_routes,
    fwd_probs,
    backward_cotangent,
    bwd_routes,
    bwd_probs,
    saved_pre,
    w_gate,
    w_up,
    w_down,
):
    experts = lax.axis_size("expert")
    sharing = min(4, experts // 2)
    exp_count = experts // sharing
    token_rows = fwd_sent.shape[1]
    top_count = fwd_routes.shape[2]
    capacity = min(token_rows, max(2, 2 * token_rows * top_count // exp_count))
    slot_count = experts * capacity
    if relay_fits(fwd_sent, top_count, capacity):
        return relay(
            fwd_sent,
            fwd_routes,
            fwd_probs,
            backward_cotangent,
            bwd_routes,
            bwd_probs,
            saved_pre,
            w_gate,
            w_up,
            w_down,
            sharing=sharing,
            capacity=capacity,
        )
    arrived = from_behind(fwd_sent, "section", 1)[0]
    gate_mat = w_gate[0]
    up_mat = w_up[0]
    down_mat = w_down[0]
    stored = saved_pre[0, 0]
    cotangent = backward_cotangent[0]
    fwd_place, fwd_weigh, fwd_count = slot_tables(fwd_routes[0], fwd_probs[0], exp_count, capacity)
    bwd_place, bwd_weigh, bwd_count = slot_tables(bwd_routes[0], bwd_probs[0], exp_count, capacity)

    def forward_rows(slot_rows):
        gate_pre = jnp.dot(slot_rows, gate_mat, preferred_element_type=jnp.float32)
        up_pre = jnp.dot(slot_rows, up_mat, preferred_element_type=jnp.float32)
        hidden_state = (jax.nn.silu(gate_pre) * up_pre).astype(jnp.bfloat16)
        return jnp.dot(hidden_state, down_mat, preferred_element_type=jnp.float32).astype(
            jnp.bfloat16
        )

    def backward_rows(slot_rows):
        contract = (((1,), (1,)), ((), ()))
        grad_hidden = lax.dot_general(
            slot_rows, down_mat, contract, preferred_element_type=jnp.float32
        )
        saved_gate = stored[:, 0].astype(jnp.float32)
        saved_up = stored[:, 1].astype(jnp.float32)
        sigma = jax.nn.sigmoid(saved_gate)
        grad_gate = (grad_hidden * saved_up * sigma * (1.0 + saved_gate * (1.0 - sigma))).astype(
            jnp.bfloat16
        )
        grad_up = (grad_hidden * saved_gate * sigma).astype(jnp.bfloat16)
        summed = lax.dot_general(grad_gate, gate_mat, contract, preferred_element_type=jnp.float32)
        summed = summed + lax.dot_general(
            grad_up, up_mat, contract, preferred_element_type=jnp.float32
        )
        return summed.astype(jnp.bfloat16)

    def send_rows(tokens, placing):
        width = tokens.shape[1]
        outgoing = jnp.dot(
            placing.T.astype(jnp.bfloat16), tokens, preferred_element_type=jnp.float32
        )
        outgoing = outgoing.astype(jnp.bfloat16).reshape(exp_count, 1, capacity, width)
        outgoing = jnp.broadcast_to(outgoing, (exp_count, sharing, capacity, width)).reshape(
            experts, capacity, width
        )
        received = lax.all_to_all(outgoing, "expert", split_axis=0, concat_axis=0, tiled=True)
        owned = jnp.zeros((), jnp.int32)
        return (received.reshape(slot_count, width), owned)

    def finish_rows(received, compute):
        width = received.shape[1]
        result_list = compute(received)
        returned = lax.all_to_all(
            result_list.reshape(experts, capacity, width),
            "expert",
            split_axis=0,
            concat_axis=0,
            tiled=True,
        )
        gathered = jnp.sum(
            returned.reshape(exp_count, sharing, capacity, width).astype(jnp.float32), axis=1
        )
        return gathered.reshape(exp_count * capacity, width)

    fwd_rows, fwd_owned = send_rows(arrived, fwd_place)
    fwd_back = finish_rows(fwd_rows, forward_rows)
    bwd_rows, bwd_owned = send_rows(cotangent, bwd_place)
    bwd_back = finish_rows(bwd_rows, backward_rows)
    fwd_next = arrived.astype(jnp.float32) + jnp.dot(
        fwd_weigh, fwd_back, precision=lax.Precision.HIGHEST
    )
    bwd_next = cotangent.astype(jnp.float32) + jnp.dot(
        bwd_weigh, bwd_back, precision=lax.Precision.HIGHEST
    )
    totals = lax.psum(fwd_count + bwd_count, ("expert", "dp"))
    expert_load = lax.dynamic_slice_in_dim(totals, lax.axis_index("expert") // sharing, 1)[0]
    return (
        fwd_next.astype(jnp.bfloat16)[None],
        bwd_next.astype(jnp.bfloat16)[None],
        expert_load.reshape(1, 1),
    )


def solution(mesh):
    in_specs = (
        P("section", ("expert", "dp"), None),
        P("section", ("expert", "dp"), None),
        P("section", ("expert", "dp"), None),
        P("section", ("expert", "dp"), None),
        P("section", ("expert", "dp"), None),
        P("section", ("expert", "dp"), None),
        P("section", "dp", None, None, "expert"),
        P("section", None, "expert"),
        P("section", None, "expert"),
        P("section", "expert", None),
    )
    out_specs = (
        P("section", ("expert", "dp"), None),
        P("section", ("expert", "dp"), None),
        P("section", "expert"),
    )
    return jax.shard_map(shards, mesh=mesh, in_specs=in_specs, out_specs=out_specs, check_vma=False)
```

```python
import functools

import jax
import jax.numpy as jnp
from jax import lax
from jax.experimental import pallas as pl
from jax.experimental.pallas import tpu as pltpu
from jax.sharding import PartitionSpec as P

MESH = pl.DeviceIdType.MESH
LEFT, RIGHT = 0, 1
FWD, BWD = 0, 1
GATHER_CHUNKS = 4
RETURN_CHUNKS = 4


def from_behind(array, axis, by):
    length = lax.axis_size(axis)
    return lax.ppermute(array, axis, [(i, (i + by) % length) for i in range(length)])


def slot_tables(routes, probs, exp_count, capacity):
    slot_count = exp_count * capacity
    flat_routes = routes.reshape(-1)
    onehot = (flat_routes[:, None] == jnp.arange(exp_count, dtype=jnp.int32)[None, :]).astype(
        jnp.int32
    )
    before = jnp.cumsum(onehot, axis=0) - onehot
    position = jnp.sum(before * onehot, axis=1)
    slot_ids = flat_routes * capacity + position
    matches = (slot_ids[:, None] == jnp.arange(slot_count, dtype=jnp.int32)[None, :]).astype(
        jnp.float32
    )
    matches = matches.reshape(routes.shape[0], routes.shape[1], slot_count)
    placing = jnp.sum(matches, axis=1)
    weighing = jnp.sum(matches * probs[:, :, None], axis=1)
    counted = jnp.sum(onehot, axis=0)
    return (placing, weighing, counted)


def cuts(width, wanted, small_first):
    unit = 256
    count = width // unit
    pieces = min(wanted, count)
    sizes = [count // pieces + (1 if i < count % pieces else 0) for i in range(pieces)]
    if small_first:
        sizes = sizes[::-1]
    starts = [sum(sizes[:i]) for i in range(pieces)]
    return [pl.ds(a * unit, b * unit) for a, b in zip(starts, sizes)]


def relay_kernel(
    size,
    x_hbm,
    cot_hbm,
    f_routes,
    b_routes,
    f_probs,
    b_probs,
    saved_hbm,
    gate_hbm,
    up_hbm,
    down_hbm,
    f_out,
    b_out,
    load_out,
    gate_w,
    up_w,
    down_w,
    saved,
    x_own,
    rows_all,
    meta,
    from_right,
    from_left,
    going,
    part,
    hidden_acc,
    grad_acc,
    mid,
    w_sem,
    shift_send,
    shift_recv,
    meta_send,
    meta_recv,
    g_send,
    g_recv,
    r_send,
    r_recv,
):
    n, n_dp, n_sec, sharing, cap, rows = size
    group = n * n_dp
    width = cot_hbm.shape[1]
    me = lax.axis_index("expert")
    dp = lax.axis_index("dp")
    sec = lax.axis_index("section")
    lin = me * n_dp + dp
    g_cuts = cuts(width, GATHER_CHUNKS, False)
    r_cuts = cuts(width, RETURN_CHUNKS, True)
    contract_last = (((1,), (1,)), ((), ()))

    def place(block):
        return pl.ds(pl.multiple_of(block * rows, rows), rows)

    own_rows = [
        pltpu.make_async_copy(x_hbm, x_own, w_sem.at[4]),
        pltpu.make_async_copy(cot_hbm, rows_all.at[BWD, place(me), :], w_sem.at[5]),
    ]
    for load in own_rows:
        load.start()
    loads = [
        pltpu.make_async_copy(down_hbm, down_w, w_sem.at[0]),
        pltpu.make_async_copy(saved_hbm, saved, w_sem.at[1]),
        pltpu.make_async_copy(gate_hbm, gate_w, w_sem.at[2]),
        pltpu.make_async_copy(up_hbm, up_w, w_sem.at[3]),
    ]
    for load in loads[:2]:
        load.start()

    barrier = pltpu.get_barrier_semaphore()

    def peer(off):
        other = lax.rem(lin + off, group)
        return {"expert": lax.div(other, n_dp), "dp": lax.rem(other, n_dp)}

    for off in range(1, group):
        pl.semaphore_signal(barrier, inc=1, device_id=peer(off), device_id_type=MESH)
    pl.semaphore_signal(
        barrier,
        inc=1,
        device_id={"section": lax.rem(sec + n_sec - 1, n_sec)},
        device_id_type=MESH,
    )

    at_row = lax.broadcasted_iota(jnp.int32, (rows, rows), 0)
    at_col = lax.broadcasted_iota(jnp.int32, (rows, rows), 1)
    eye = at_row == at_col

    def column(line):
        spread = jnp.where(eye, jnp.broadcast_to(line, (rows, rows)), 0.0)
        return jnp.sum(spread, axis=1, keepdims=True)

    meta[lin] = jnp.zeros(meta.shape[1:], jnp.float32)
    for span, routes in ((FWD, f_routes), (BWD, b_routes)):
        named_row = routes[...].astype(jnp.float32)
        named = column(named_row)
        earlier = jnp.where((named == named_row) & (at_row < at_col), 1.0, 0.0)
        slot = named_row * cap + jnp.sum(earlier, axis=0, keepdims=True)
        meta[lin, span : span + 1, 0:rows] = slot
    pl.semaphore_wait(barrier, group)

    def gather_copy(span, way, hop, chunk):
        block = me - (hop - 1) if way == RIGHT else me + (hop - 1)
        there = me + 1 if way == RIGHT else me - 1
        piece = rows_all.at[span, place(block), g_cuts[chunk]]
        return pltpu.make_async_remote_copy(
            src_ref=piece,
            dst_ref=piece,
            send_sem=g_send.at[span, way, hop - 1, chunk],
            recv_sem=g_recv.at[span, way, hop - 1, chunk],
            device_id={"expert": there},
            device_id_type=MESH,
        )

    def gather_sends(way, hop):
        if way == RIGHT:
            return (me >= hop - 1) & (me < n - 1)
        return (me <= n - hop) & (me > 0)

    def gather_wait(span, way, hop, chunk):
        block = me - hop if way == RIGHT else me + hop
        there = me - 1 if way == RIGHT else me + 1
        piece = rows_all.at[span, place(block), g_cuts[chunk]]
        pltpu.make_async_remote_copy(
            src_ref=piece,
            dst_ref=piece,
            send_sem=g_send.at[span, way, hop - 1, chunk],
            recv_sem=g_recv.at[span, way, hop - 1, chunk],
            device_id={"expert": there},
            device_id_type=MESH,
        ).wait_recv()

    def gather_start(span, hop, chunk):
        for way in (LEFT, RIGHT):

            @pl.when(gather_sends(way, hop))
            def _():
                gather_copy(span, way, hop, chunk).start()

    inner = (me > 0) & (me < n - 1)

    def gather_step(span, hop, chunk):
        for way in (LEFT, RIGHT):
            there = me >= hop if way == RIGHT else me + hop < n

            @pl.when(there & inner)
            def _():
                gather_wait(span, way, hop, chunk)

            if hop < n - 1:

                @pl.when(gather_sends(way, hop + 1))
                def _():
                    gather_copy(span, way, hop + 1, chunk).start()

    def gather_rest(span, chunk):
        @pl.when(me == 0)
        def _():
            for hop in range(1, n):
                gather_wait(span, LEFT, hop, chunk)

        @pl.when(me == n - 1)
        def _():
            for hop in range(1, n):
                gather_wait(span, RIGHT, hop, chunk)

    def return_copy(span, way, block, chunk):
        landing = from_left if way == RIGHT else from_right
        there = me + 1 if way == RIGHT else me - 1
        spot = pl.ds(block * rows, rows)
        return pltpu.make_async_remote_copy(
            src_ref=going.at[span, spot, r_cuts[chunk]],
            dst_ref=landing.at[span, spot, r_cuts[chunk]],
            send_sem=r_send.at[span, way, block, chunk],
            recv_sem=r_recv.at[span, way, block, chunk],
            device_id={"expert": there},
            device_id_type=MESH,
        )

    def return_wait(span, way, block, chunk):
        landing = from_left if way == RIGHT else from_right
        there = me - 1 if way == RIGHT else me + 1
        piece = landing.at[span, place(block), r_cuts[chunk]]
        pltpu.make_async_remote_copy(
            src_ref=piece,
            dst_ref=piece,
            send_sem=r_send.at[span, way, block, chunk],
            recv_sem=r_recv.at[span, way, block, chunk],
            device_id={"expert": there},
            device_id_type=MESH,
        ).wait_recv()

    def return_step(span, hop, chunk, nth):
        for way in (LEFT, RIGHT):
            at = n - 1 - hop if way == LEFT else hop
            block = nth if way == LEFT else n - 1 - nth
            landing = from_left if way == RIGHT else from_right

            @pl.when(me == at)
            def _():
                spot = pl.ds(block * rows, rows)
                total = part[span, spot, r_cuts[chunk]]
                if hop > 0:
                    return_wait(span, way, block, chunk)
                    total = total + landing[span, spot, r_cuts[chunk]].astype(jnp.float32)
                going[span, spot, r_cuts[chunk]] = total.astype(jnp.bfloat16)
                return_copy(span, way, block, chunk).start()

    onward = [(nth, hop) for nth in range(n - 1) for hop in range(1, n - 1 - nth)]

    def finish(span, chunk, base, probs, out):
        spot = place(me)
        for way in (LEFT, RIGHT):
            landing = from_left if way == RIGHT else from_right
            there = me > 0 if way == RIGHT else me < n - 1

            @pl.when(there)
            def _():
                return_wait(span, way, me, chunk)
                part[span, spot, r_cuts[chunk]] += landing[span, spot, r_cuts[chunk]].astype(
                    jnp.float32
                )

        out[:, r_cuts[chunk]] = (
            base(r_cuts[chunk]).astype(jnp.float32)
            + column(probs[...]) * part[span, spot, r_cuts[chunk]]
        )

    def meta_copy(off):
        return pltpu.make_async_remote_copy(
            src_ref=meta.at[lin],
            dst_ref=meta.at[lin],
            send_sem=meta_send.at[off],
            recv_sem=meta_recv.at[off],
            device_id=peer(off),
            device_id_type=MESH,
        )

    def meta_wait(off):
        other = meta.at[lax.rem(lin + group - off, group)]
        pltpu.make_async_remote_copy(
            src_ref=other,
            dst_ref=other,
            send_sem=meta_send.at[off],
            recv_sem=meta_recv.at[off],
            device_id=peer(group - off),
            device_id_type=MESH,
        ).wait_recv()

    def shift_copy(chunk):
        return pltpu.make_async_remote_copy(
            src_ref=x_own.at[:, g_cuts[chunk]],
            dst_ref=rows_all.at[FWD, place(me), g_cuts[chunk]],
            send_sem=shift_send.at[chunk],
            recv_sem=shift_recv.at[chunk],
            device_id={"section": lax.rem(sec + 1, n_sec)},
            device_id_type=MESH,
        )

    own_rows[0].wait()
    for chunk in range(len(g_cuts)):
        shift_copy(chunk).start()
    own_rows[1].wait()
    for chunk in range(len(g_cuts)):
        gather_start(BWD, 1, chunk)
    for load in loads[2:]:
        load.start()
    for off in range(1, group):
        meta_copy(off).start()

    for hop in range(1, n - 1):
        for chunk in range(len(g_cuts)):
            gather_step(BWD, hop, chunk)
        if hop == n - 2:
            for chunk in range(len(g_cuts)):
                shift_copy(chunk).wait_recv()
                gather_start(FWD, 1, chunk)
            for off in range(1, group):
                meta_wait(off)
            first = (lax.div(me, sharing) * cap).astype(jnp.float32)
            owned = jnp.zeros((2, rows), jnp.float32)
            for other in range(group):
                slots = meta[other, 0:2, 0:rows] - first
                owned = owned + jnp.where((slots >= 0.0) & (slots < cap), 1.0, 0.0)
            owned = jnp.sum(jnp.sum(owned, axis=1, keepdims=True), axis=0, keepdims=True)
            load_out[...] = owned.astype(jnp.int32)

            def slots_of(span, block):
                line = meta[block * n_dp + dp, span : span + 1, 0:rows] - first
                return column(line)

            lanes = lax.broadcasted_iota(jnp.int32, (rows, n * cap), 1).astype(jnp.float32)
            taken = []
            for block in range(n):
                slots = slots_of(BWD, block)
                hit = (slots >= 0.0) & (slots < cap) & (lanes == slots + block * cap)
                taken.append(jnp.where(hit, 1.0, 0.0))
            taken = jnp.concatenate(taken, axis=0).astype(jnp.bfloat16)
            kept = []
            for block in range(n):
                slots = slots_of(FWD, block)
                kept.append(jnp.where((slots >= 0.0) & (slots < cap), 1.0, 0.0))
            kept = jnp.concatenate(kept, axis=0) > 0.5
            loads[1].wait()
            stored = saved[...].astype(jnp.float32)
            saved_gate = jnp.dot(
                taken, stored[:, 0, :].astype(jnp.bfloat16), preferred_element_type=jnp.float32
            )
            saved_up = jnp.dot(
                taken, stored[:, 1, :].astype(jnp.bfloat16), preferred_element_type=jnp.float32
            )
            sigma = jax.nn.sigmoid(saved_gate)
            hidden_acc[0] = saved_up * sigma * (1.0 + saved_gate * (1.0 - sigma))
            hidden_acc[1] = saved_gate * sigma

    loads[0].wait()
    for chunk, cut in enumerate(g_cuts):
        gather_rest(BWD, chunk)
        term = lax.dot_general(
            down_w[:, cut],
            rows_all[BWD, :, cut],
            contract_last,
            preferred_element_type=jnp.float32,
        )
        if chunk == 0:
            grad_acc[...] = term
        else:
            grad_acc[...] += term
    grad_hidden = grad_acc[...].T
    mid[0] = (grad_hidden * hidden_acc[0]).astype(jnp.bfloat16)
    mid[1] = (grad_hidden * hidden_acc[1]).astype(jnp.bfloat16)

    loads[2].wait()
    loads[3].wait()

    def bwd_part(chunk):
        cut = r_cuts[chunk]
        turned = lax.dot_general(
            gate_w[cut, :], mid[0], contract_last, preferred_element_type=jnp.float32
        ) + lax.dot_general(
            up_w[cut, :], mid[1], contract_last, preferred_element_type=jnp.float32
        )
        part[BWD, :, cut] = turned.T

    r_count, g_count = len(r_cuts), len(g_cuts)
    for chunk in range(max(r_count, g_count)):
        if chunk < r_count:
            bwd_part(chunk)
            return_step(BWD, 0, chunk, 0)
        if chunk < g_count:
            gather_step(FWD, 1, chunk)
    for nth in range(1, n - 1):
        for chunk in range(r_count):
            return_step(BWD, 0, chunk, nth)
    for hop in range(1, n - 2):
        for chunk in range(max(r_count, g_count)):
            if chunk < g_count:
                gather_step(FWD, hop + 1, chunk)
            if chunk < r_count:
                return_step(BWD, hop, chunk, 0)
    late = [(nth, hop) for nth, hop in onward if nth > 0 or hop == n - 2]

    for chunk, cut in enumerate(g_cuts):
        gather_rest(FWD, chunk)
        for at, weights in ((0, gate_w), (1, up_w)):
            term = jnp.dot(
                rows_all[FWD, :, cut], weights[cut, :], preferred_element_type=jnp.float32
            )
            if chunk == 0:
                hidden_acc[at] = term
            else:
                hidden_acc[at] += term
        if chunk < r_count:
            for nth, hop in late:
                return_step(BWD, hop, chunk, nth)
    for chunk in range(g_count, r_count):
        for nth, hop in late:
            return_step(BWD, hop, chunk, nth)
    activated = jax.nn.silu(hidden_acc[0]) * hidden_acc[1]
    mid[0] = jnp.where(kept, activated, 0.0).astype(jnp.bfloat16)

    for chunk in range(r_count):
        cut = r_cuts[chunk]
        part[FWD, :, cut] = jnp.dot(mid[0], down_w[:, cut], preferred_element_type=jnp.float32)
        return_step(FWD, 0, chunk, 0)
    for nth in range(1, n - 1):
        for chunk in range(r_count):
            return_step(FWD, 0, chunk, nth)
    for nth, hop in onward:
        if nth == 0:
            for chunk in range(r_count):
                return_step(FWD, hop, chunk, nth)
    for chunk in range(r_count):
        finish(BWD, chunk, lambda cut: rows_all[BWD, place(me), cut], b_probs, b_out)
    for nth, hop in onward:
        if nth > 0:
            for chunk in range(r_count):
                return_step(FWD, hop, chunk, nth)
    for chunk in range(r_count):
        finish(FWD, chunk, lambda cut: rows_all[FWD, place(me), cut], f_probs, f_out)

    for chunk in range(len(g_cuts)):
        shift_copy(chunk).wait_send()
    for off in range(1, group):
        meta_copy(off).wait_send()
    for span in (BWD, FWD):
        for way in (LEFT, RIGHT):
            for hop in range(1, n):

                @pl.when(gather_sends(way, hop))
                def _():
                    for chunk in range(len(g_cuts)):
                        gather_copy(span, way, hop, chunk).wait_send()

            for block in range(n):

                @pl.when(me > block if way == LEFT else me < block)
                def _():
                    for chunk in range(r_count):
                        return_copy(span, way, block, chunk).wait_send()


def relay_fits(fwd_sent, top_count, capacity):
    rows, width = fwd_sent.shape[1:]
    return (
        top_count == 1
        and capacity == rows
        and rows % 16 == 0
        and rows <= 128
        and width % 256 == 0
        and lax.axis_size("expert") > 2
        and lax.axis_size("section") > 1
    )


def relay(
    fwd_sent,
    fwd_routes,
    fwd_probs,
    backward_cotangent,
    bwd_routes,
    bwd_probs,
    saved_pre,
    w_gate,
    w_up,
    w_down,
    *,
    sharing,
    capacity,
):
    n, n_dp, n_sec = (lax.axis_size(name) for name in ("expert", "dp", "section"))
    rows, width = fwd_sent.shape[1:]
    hidden = w_gate.shape[2]
    tokens = n * rows
    bf16, f32 = jnp.bfloat16, jnp.float32
    group = n * n_dp
    g_count = len(cuts(width, GATHER_CHUNKS, False))
    r_count = len(cuts(width, RETURN_CHUNKS, True))
    vmem = pl.BlockSpec(memory_space=pltpu.VMEM)
    hbm = pl.BlockSpec(memory_space=pl.ANY)
    f_next, b_next, load = pl.pallas_call(
        functools.partial(relay_kernel, (n, n_dp, n_sec, sharing, capacity, rows)),
        out_shape=(
            jax.ShapeDtypeStruct((rows, width), f32),
            jax.ShapeDtypeStruct((rows, width), f32),
            jax.ShapeDtypeStruct((1, 1), jnp.int32),
        ),
        in_specs=[hbm] * 2 + [vmem] * 4 + [hbm] * 4,
        out_specs=(vmem, vmem, vmem),
        scratch_shapes=[
            pltpu.VMEM((width, hidden), bf16),
            pltpu.VMEM((width, hidden), bf16),
            pltpu.VMEM((hidden, width), bf16),
            pltpu.VMEM(saved_pre.shape[2:], bf16),
            pltpu.VMEM((rows, width), bf16),
            pltpu.VMEM((2, tokens, width), bf16),
            pltpu.VMEM((group, 8, 128), f32),
            pltpu.VMEM((2, tokens, width), bf16),
            pltpu.VMEM((2, tokens, width), bf16),
            pltpu.VMEM((2, tokens, width), bf16),
            pltpu.VMEM((2, tokens, width), f32),
            pltpu.VMEM((2, tokens, hidden), f32),
            pltpu.VMEM((hidden, tokens), f32),
            pltpu.VMEM((2, tokens, hidden), bf16),
            pltpu.SemaphoreType.DMA((6,)),
            pltpu.SemaphoreType.DMA((g_count,)),
            pltpu.SemaphoreType.DMA((g_count,)),
            pltpu.SemaphoreType.DMA((group,)),
            pltpu.SemaphoreType.DMA((group,)),
            pltpu.SemaphoreType.DMA((2, 2, n - 1, g_count)),
            pltpu.SemaphoreType.DMA((2, 2, n - 1, g_count)),
            pltpu.SemaphoreType.DMA((2, 2, n, r_count)),
            pltpu.SemaphoreType.DMA((2, 2, n, r_count)),
        ],
        compiler_params=pltpu.CompilerParams(
            collective_id=0, has_side_effects=True, vmem_limit_bytes=60 * 1024 * 1024
        ),
        cost_estimate=pl.CostEstimate(
            flops=12 * tokens * width * hidden,
            bytes_accessed=6 * width * hidden,
            transcendentals=2 * tokens * hidden,
        ),
    )(
        fwd_sent[0],
        backward_cotangent[0],
        fwd_routes.reshape(1, rows),
        bwd_routes.reshape(1, rows),
        fwd_probs.reshape(1, rows),
        bwd_probs.reshape(1, rows),
        saved_pre[0, 0],
        w_gate[0],
        w_up[0],
        w_down[0],
    )
    return f_next.astype(bf16)[None], b_next.astype(bf16)[None], load


def shards(
    fwd_sent,
    fwd_routes,
    fwd_probs,
    backward_cotangent,
    bwd_routes,
    bwd_probs,
    saved_pre,
    w_gate,
    w_up,
    w_down,
):
    experts = lax.axis_size("expert")
    sharing = min(4, experts // 2)
    exp_count = experts // sharing
    token_rows = fwd_sent.shape[1]
    top_count = fwd_routes.shape[2]
    capacity = min(token_rows, max(2, 2 * token_rows * top_count // exp_count))
    slot_count = experts * capacity
    if relay_fits(fwd_sent, top_count, capacity):
        return relay(
            fwd_sent,
            fwd_routes,
            fwd_probs,
            backward_cotangent,
            bwd_routes,
            bwd_probs,
            saved_pre,
            w_gate,
            w_up,
            w_down,
            sharing=sharing,
            capacity=capacity,
        )
    arrived = from_behind(fwd_sent, "section", 1)[0]
    gate_mat = w_gate[0]
    up_mat = w_up[0]
    down_mat = w_down[0]
    stored = saved_pre[0, 0]
    cotangent = backward_cotangent[0]
    fwd_place, fwd_weigh, fwd_count = slot_tables(fwd_routes[0], fwd_probs[0], exp_count, capacity)
    bwd_place, bwd_weigh, bwd_count = slot_tables(bwd_routes[0], bwd_probs[0], exp_count, capacity)

    def forward_rows(slot_rows):
        gate_pre = jnp.dot(slot_rows, gate_mat, preferred_element_type=jnp.float32)
        up_pre = jnp.dot(slot_rows, up_mat, preferred_element_type=jnp.float32)
        hidden_state = (jax.nn.silu(gate_pre) * up_pre).astype(jnp.bfloat16)
        return jnp.dot(hidden_state, down_mat, preferred_element_type=jnp.float32).astype(
            jnp.bfloat16
        )

    def backward_rows(slot_rows):
        contract = (((1,), (1,)), ((), ()))
        grad_hidden = lax.dot_general(
            slot_rows, down_mat, contract, preferred_element_type=jnp.float32
        )
        saved_gate = stored[:, 0].astype(jnp.float32)
        saved_up = stored[:, 1].astype(jnp.float32)
        sigma = jax.nn.sigmoid(saved_gate)
        grad_gate = (grad_hidden * saved_up * sigma * (1.0 + saved_gate * (1.0 - sigma))).astype(
            jnp.bfloat16
        )
        grad_up = (grad_hidden * saved_gate * sigma).astype(jnp.bfloat16)
        summed = lax.dot_general(grad_gate, gate_mat, contract, preferred_element_type=jnp.float32)
        summed = summed + lax.dot_general(
            grad_up, up_mat, contract, preferred_element_type=jnp.float32
        )
        return summed.astype(jnp.bfloat16)

    def send_rows(tokens, placing):
        width = tokens.shape[1]
        outgoing = jnp.dot(
            placing.T.astype(jnp.bfloat16), tokens, preferred_element_type=jnp.float32
        )
        outgoing = outgoing.astype(jnp.bfloat16).reshape(exp_count, 1, capacity, width)
        outgoing = jnp.broadcast_to(outgoing, (exp_count, sharing, capacity, width)).reshape(
            experts, capacity, width
        )
        received = lax.all_to_all(outgoing, "expert", split_axis=0, concat_axis=0, tiled=True)
        owned = jnp.zeros((), jnp.int32)
        return (received.reshape(slot_count, width), owned)

    def finish_rows(received, compute):
        width = received.shape[1]
        result_list = compute(received)
        returned = lax.all_to_all(
            result_list.reshape(experts, capacity, width),
            "expert",
            split_axis=0,
            concat_axis=0,
            tiled=True,
        )
        gathered = jnp.sum(
            returned.reshape(exp_count, sharing, capacity, width).astype(jnp.float32), axis=1
        )
        return gathered.reshape(exp_count * capacity, width)

    fwd_rows, fwd_owned = send_rows(arrived, fwd_place)
    fwd_back = finish_rows(fwd_rows, forward_rows)
    bwd_rows, bwd_owned = send_rows(cotangent, bwd_place)
    bwd_back = finish_rows(bwd_rows, backward_rows)
    fwd_next = arrived.astype(jnp.float32) + jnp.dot(
        fwd_weigh, fwd_back, precision=lax.Precision.HIGHEST
    )
    bwd_next = cotangent.astype(jnp.float32) + jnp.dot(
        bwd_weigh, bwd_back, precision=lax.Precision.HIGHEST
    )
    totals = lax.psum(fwd_count + bwd_count, ("expert", "dp"))
    expert_load = lax.dynamic_slice_in_dim(totals, lax.axis_index("expert") // sharing, 1)[0]
    return (
        fwd_next.astype(jnp.bfloat16)[None],
        bwd_next.astype(jnp.bfloat16)[None],
        expert_load.reshape(1, 1),
    )


def solution(mesh):
    in_specs = (
        P("section", ("expert", "dp"), None),
        P("section", ("expert", "dp"), None),
        P("section", ("expert", "dp"), None),
        P("section", ("expert", "dp"), None),
        P("section", ("expert", "dp"), None),
        P("section", ("expert", "dp"), None),
        P("section", "dp", None, None, "expert"),
        P("section", None, "expert"),
        P("section", None, "expert"),
        P("section", "expert", None),
    )
    out_specs = (
        P("section", ("expert", "dp"), None),
        P("section", ("expert", "dp"), None),
        P("section", "expert"),
    )
    return jax.shard_map(shards, mesh=mesh, in_specs=in_specs, out_specs=out_specs, check_vma=False)
```
